32 devices in a mesh: shard: 16 (over z, x, core), rep: 2 (over y).
Axes of the slice: x: 2, y: 2, z: 4, core: 2. Of those that a mesh axis runs over, the one named last changes fastest.
Arguments:
- layer_input: bfloat16 [32768, 1024], P(('shard', 'rep')), may hold values from -6 to 6
- attention_gain: float32 [1024], replicated, may hold values from 0.1 to 1.9
- query_weight: bfloat16 [1024, 1024], P('shard'), may hold values from -0.25 to 0.25
- key_weight: bfloat16 [1024, 512], P('shard'), may hold values from -0.25 to 0.25
- value_weight: bfloat16 [1024, 512], P('shard'), may hold values from -0.1875 to 0.1875
- output_weight: bfloat16 [1024, 1024], P('shard'), may hold values from -0.75 to 0.75
- expert_gain: float32 [1024], replicated, may hold values from 0.1 to 1.9
- router_weight: bfloat16 [1024, 32], replicated, may hold values from -0.08984375 to 0.08984375
- gate_weight: bfloat16 [32, 1024, 512], P('shard'), may hold values from -0.1875 to 0.1875
- up_weight: bfloat16 [32, 1024, 512], P('shard'), may hold values from -0.1875 to 0.1875
- down_weight: bfloat16 [32, 512, 1024], P('shard'), may hold values from -0.25 to 0.25
- lengths: int32 [32], P(('shard', 'rep')), may hold values from 512 to 1024, as said below
- routes: int32 [32768, 8], P(('shard', 'rep')), may hold values from 0 to 31, all different within a row; in each aligned block of 1024 rows (0 to 1023, 1024 to 2047, ...) at most 288 rows name the same one
- cotangent: bfloat16 [32768, 1024], P(('shard', 'rep')), may hold values from -6 to 6
Outputs:
- layer_output: bfloat16 [32768, 1024], P(('shard', 'rep'))
- input_gradient: bfloat16 [32768, 1024], P(('shard', 'rep'))
- attention_gain_gradient: float32 [1024], replicated
- query_weight_gradient: float32 [1024, 1024], P('shard')
- key_weight_gradient: float32 [1024, 512], P('shard')
- value_weight_gradient: float32 [1024, 512], P('shard')
- output_weight_gradient: float32 [1024, 1024], P('shard')
- expert_gain_gradient: float32 [1024], replicated
- router_weight_gradient: float32 [1024, 32], replicated
- gate_weight_gradient: float32 [32, 1024, 512], P('shard')
- up_weight_gradient: float32 [32, 1024, 512], P('shard')
- down_weight_gradient: float32 [32, 512, 1024], P('shard')
The draws below stay inside these ranges and needn't reach their ends.
Inputs may be any that keep to these rules, and one draw needn't show every extreme that they name: `lengths`: every slot holds one sequence from position 0; some slot is filled to its end and some holds exactly 512 tokens. `routes`: A token's 8 experts are distinct; among the 1024 rows of one device no expert is named more than 288 times.
All inputs are finite; a program needn't handle non-finite values.
Results may differ from the reference program's by a relative error of at most 0.015.
The reference program's roundings to bfloat16 on the way count: a program that leaves them out, or rounds other values in their place, can miss the bound.
Values may be sent and summed in bfloat16 or wider, within the bound.
A program may use at most 448 MiB of HBM per device.

```python
import math
import jax
import jax.numpy as jnp
import numpy as np
from jax import lax

D = 1024
HEADS = 16
KV = 8
HD = 64
EXPERTS = 32
FF = 512
TOP = 8
SLOT = 1024
CAP = 288
SLOTS = 32
TOKENS = 32768


def draw_lengths(key, part):
    key = jax.random.fold_in(key, 7)
    first_key, second_key = jax.random.split(key)
    drawn = jax.random.randint(first_key, (SLOTS,), SLOT // 2, SLOT + 1)
    order = jax.random.permutation(second_key, SLOTS)
    drawn = jnp.where(order == 0, SLOT, drawn)
    drawn = jnp.where(order == 1, SLOT // 2, drawn)
    return drawn.astype(jnp.int32)


def with_spikes(array, key, source, target, shards_of, factor):
    def block_of(dim):
        return (jnp.arange(array.shape[dim]) // (array.shape[dim] // shards_of)).reshape((-1,) + (1,) * (array.ndim - 1 - dim))

    first = jax.random.permutation(key, shards_of)[block_of(target)]
    second = (block_of(target) + shards_of // 2) % shards_of
    return jnp.where((block_of(source) == first) | (block_of(source) == second), factor * array, array)


def level_of(own_key, extent, pieces, smallest, high):
    level, own = 1.0, jax.random.fold_in(own_key, 6)
    for dim, blocks in pieces:
        steps = jnp.exp(jax.random.uniform(jax.random.fold_in(own, dim), (blocks,), jnp.float32, smallest / len(pieces), high / len(pieces)))
        level = level * jnp.repeat(steps, extent[dim] // blocks).reshape([-1 if axis == dim else 1 for axis in range(len(extent))])
    return level


def assign_block(rng, own, number, rows, number_of, top, limit, lean):
    order = jax.random.permutation(rng, number_of)
    heavy_load, common = load_shares(number_of, rows * top, limit, lean, True), load_shares(number_of, rows * top, limit, lean, False)
    places = jnp.arange(number_of)

    def named(sizes, offset_by):
        used = int((sizes > 0).sum())
        fixed = max(1, used // 4)
        passed = fixed + (places - fixed + offset_by * (used - fixed)) % max(1, number_of - fixed)
        return jnp.zeros((number_of,), jnp.int32).at[order[jnp.where(places < fixed, places, passed)]].set(jnp.asarray(sizes, jnp.int32))

    sizes = jnp.where(number % 4 == 0, named(heavy_load, number // 4), named(common, number - number // 4 - 1))
    mixed = jax.random.permutation(jax.random.fold_in(own, 3), number_of)
    source_of, receiver = mixed[0:number_of // 2 * 2:2], mixed[1:number_of // 2 * 2:2]
    slack = jnp.minimum(sizes[source_of] - 1, limit - sizes[receiver]) // 2
    slack = jnp.where((source_of == order[0]) | (receiver == order[0]) | (sizes[receiver] == 0), 0, jnp.maximum(slack, 0))
    passed = jax.random.randint(jax.random.fold_in(own, 4), (number_of // 2,), 0, 1 << 20) % (slack + 1)
    sizes = sizes.at[source_of].add(-passed).at[receiver].add(passed)
    items = jnp.searchsorted(jnp.cumsum(sizes), jnp.arange(rows * top), side="right").astype(jnp.int32)
    listing = items.reshape(top, rows).T
    listing = listing[jax.random.permutation(jax.random.fold_in(own, 1), rows)]
    offset_by = jax.random.randint(jax.random.fold_in(own, 2), (rows, 1), 0, top)
    return jnp.take_along_axis(listing, (jnp.arange(top)[None, :] + offset_by) % top, axis=1)


def load_shares(count, total, most, lean, full):
    loads = [(1 << 20) // math.isqrt(standing ** lean) + 1 for standing in range(1, count + 1)]
    largest = most if full else min(most, max(-(-total // count), total * loads[0] // sum(loads)))
    least = 1 if total - largest >= count - 1 else 0
    holding, surplus = [largest] + [least] * (count - 1), total - largest - least * (count - 1)
    while surplus > 0:
        movable = [i for i in range(1, count) if holding[i] < largest] or [i for i in range(1, count) if holding[i] < most]
        pool, left = sum([loads[i] for i in movable]), surplus
        for i in movable:
            addition = min(most - holding[i], max(1, left * loads[i] // pool), surplus)
            holding[i] = holding[i] + addition
            surplus = surplus - addition
    return np.array(holding)


def bell_draw(key, shape, spread, bound, shards=(), held_as=jnp.bfloat16):
    level = level_of(key, shape, shards, -0.22, 0.18) if shards else 1.0
    entries = jax.random.normal(key, shape, jnp.float32) * spread * level
    return jnp.minimum(jnp.maximum(entries, -bound), bound).astype(held_as)


def noise_with(rng, extent, scale, most, cuts, heavy, kind=jnp.bfloat16):
    entries = scale * jax.random.normal(rng, extent, jnp.float32)
    if cuts:
        entries = entries * level_of(rng, extent, cuts, -0.22, 0.18)
    return jnp.clip(with_spikes(entries, jax.random.fold_in(rng, 3), *heavy), -most, most).astype(kind)


def setup_inputs(seed: int = 0) -> dict:
    splits = jax.random.split(jax.random.key(seed), 15)
    layer_input = bell_draw(splits[0], (TOKENS, D), 1.0, 6.0, ((0, 32),))
    attention_gain = jnp.clip(1.0 + 0.18 * jax.random.normal(splits[1], (D,), jnp.float32), 0.1, 1.9)
    query_weight = bell_draw(splits[2], (D, HEADS * HD), (D // 2) ** -0.5, 0.25, ((0, 16),))
    key_weight = bell_draw(splits[3], (D, KV * HD), (D // 2) ** -0.5, 0.25, ((0, 16),))
    value_weight = bell_draw(splits[4], (D, KV * HD), D ** -0.5, 0.1875, ((0, 16),))
    output_weight = bell_draw(splits[5], (HEADS * HD, D), HD ** -0.5, 0.75, ((0, 16),))
    expert_gain = jnp.clip(1.0 + 0.18 * jax.random.normal(splits[6], (D,), jnp.float32), 0.1, 1.9)
    router_weight = bell_draw(splits[7], (D, EXPERTS), 0.0156, 0.08984375)
    gate_weight = bell_draw(splits[8], (EXPERTS, D, FF), D ** -0.5, 0.1875, ((0, 16),))
    up_weight = bell_draw(splits[9], (EXPERTS, D, FF), D ** -0.5, 0.1875, ((0, 16),))
    down_weight = bell_draw(splits[10], (EXPERTS, FF, D), FF ** -0.5, 0.25, ((0, 16),))
    lengths = draw_lengths(jax.random.fold_in(splits[14], 71), 0)
    routes_keys = jax.random.split(jax.random.fold_in(splits[12], 1), TOKENS // SLOT)
    routes_turns = jax.random.permutation(jax.random.fold_in(splits[12], 3), TOKENS // SLOT)
    routes = jax.vmap(lambda own, number: assign_block(jax.random.fold_in(splits[12], 2), own, number, SLOT, EXPERTS, TOP, CAP, 1))(routes_keys, routes_turns).reshape((TOKENS, TOP))
    cotangent = noise_with(splits[13], (TOKENS, D), 1.0, 6.0, ((0, 32),), (0, 1, 32, 2.75))
    return {"layer_input": layer_input, "attention_gain": attention_gain, "query_weight": query_weight, "key_weight": key_weight, "value_weight": value_weight, "output_weight": output_weight, "expert_gain": expert_gain, "router_weight": router_weight, "gate_weight": gate_weight, "up_weight": up_weight, "down_weight": down_weight, "lengths": lengths, "routes": routes, "cotangent": cotangent}


@jax.custom_vjp
def low(v):
    return lax.optimization_barrier(v.astype(jnp.bfloat16)).astype(jnp.float32)

@jax.custom_vjp
def low_back(v):
    return v

def low_keep(v):
    return (low(v), None)

def low_pass(kept, grad):
    return (grad,)

def back_keep(v):
    return (v, None)

def back_low(kept, grad):
    return (low(grad),)
low.defvjp(low_keep, low_pass)
low_back.defvjp(back_keep, back_low)
epsilon = 1e-06
masked_score = -1e+30
rotary_base = 10000.0

def highest_dot(left, right):
    return jnp.dot(left, right, preferred_element_type=jnp.float32, precision=lax.Precision.HIGHEST)

def normalize(values, gain):
    factor = lax.rsqrt(lax.optimization_barrier(jnp.mean(values * values, axis=-1, keepdims=True)) + epsilon)
    return values * factor * gain

def softmax_last(values):
    maximum = lax.optimization_barrier(jnp.max(values, axis=-1, keepdims=True))
    powered = jnp.exp(values - maximum)
    return powered / lax.optimization_barrier(jnp.sum(powered, axis=-1, keepdims=True))

def rope_tables(length_rows, head_width):
    halfway = head_width // 2
    index_float = jnp.arange(halfway, dtype=jnp.float32)
    frequency = jnp.exp(-jnp.log(rotary_base) * index_float * 2.0 / head_width)
    angle = jnp.arange(length_rows, dtype=jnp.float32)[:, None] * frequency[None, :]
    return (jnp.cos(angle)[:, None, :], jnp.sin(angle)[:, None, :])

def rotate(values, cosine, sine):
    halfway = values.shape[-1] // 2
    first_half = values[..., :halfway]
    second_half = values[..., halfway:]
    return jnp.concatenate([first_half * cosine - second_half * sine, second_half * cosine + first_half * sine], axis=-1)

def layer(inputs_f, weights, lengths, routes):
    attention_gain, query_weight, key_weight, value_weight, output_weight, expert_gain, router_weight, gate_weight, up_weight, down_weight = weights
    groups = HEADS // KV
    scale = HD ** (-0.5)

    def slot_layer(packed):
        slot_input, length, slot_routes = packed
        normed_one = low(normalize(slot_input, attention_gain))
        cosine, sine = rope_tables(SLOT, HD)
        query_pre = low_back(highest_dot(normed_one, query_weight))
        key_pre = low_back(highest_dot(normed_one, key_weight))
        values = low(low_back(highest_dot(normed_one, value_weight))).reshape(SLOT, KV, HD)
        queries = low(rotate(query_pre.reshape(SLOT, HEADS, HD), cosine, sine)).reshape(SLOT, KV, groups, HD)
        keys = low(rotate(key_pre.reshape(SLOT, KV, HD), cosine, sine))
        scores = jnp.einsum('qhgd,khd->hgqk', queries, keys, precision=lax.Precision.HIGHEST) * scale
        scores = low_back(scores)
        places = jnp.arange(SLOT, dtype=jnp.int32)
        allowed = (places[None, :] <= places[:, None]) & (places[None, :] < length)
        scores = jnp.where(allowed[None, None], scores, masked_score)
        weights_soft = softmax_last(scores)
        mixed = jnp.einsum('hgqk,khd->qhgd', low(weights_soft), values, precision=lax.Precision.HIGHEST)
        attended = low(low_back(mixed.reshape(SLOT, HEADS * HD)))
        branch = low_back(highest_dot(attended, output_weight))
        residual = slot_input + branch
        normed_two = low(normalize(residual, expert_gain))
        logits = low_back(highest_dot(normed_two, router_weight))
        chosen = jnp.take_along_axis(logits, slot_routes, axis=1)
        gates = softmax_last(chosen)
        assigned = slot_routes.reshape(-1).astype(jnp.int32)
        marks = (assigned[:, None] == jnp.arange(EXPERTS, dtype=jnp.int32)[None, :]).astype(jnp.int32)
        ranked = lax.optimization_barrier(jnp.sum((jnp.cumsum(marks, axis=0) - marks) * marks, axis=1)).astype(jnp.int32)
        targets = (assigned * CAP + ranked).astype(jnp.int32)
        spread_rows = jnp.broadcast_to(normed_two[:, None, :], (SLOT, TOP, D)).reshape(SLOT * TOP, D)
        buffer = jnp.zeros((EXPERTS * CAP, D), jnp.float32).at[targets].set(spread_rows)
        expert_rows = low_back(buffer).reshape(EXPERTS, CAP, D)
        gate_part = low_back(jnp.einsum('erd,edf->erf', expert_rows, gate_weight, precision=lax.Precision.HIGHEST))
        up_part = low_back(jnp.einsum('erd,edf->erf', expert_rows, up_weight, precision=lax.Precision.HIGHEST))
        hidden = low(gate_part * jax.nn.sigmoid(gate_part) * up_part)
        expert_out = low(low_back(jnp.einsum('erf,efd->erd', hidden, down_weight, precision=lax.Precision.HIGHEST)))
        picked = expert_out.reshape(EXPERTS * CAP, D)[targets].reshape(SLOT, TOP, D)
        mixture = lax.optimization_barrier(jnp.sum(gates[:, :, None] * picked, axis=1))
        return residual + mixture
    slot_inputs = inputs_f.reshape(SLOTS, SLOT, D)
    slot_routes_all = routes.reshape(SLOTS, SLOT, TOP)
    outputs = lax.map(jax.checkpoint(slot_layer), (slot_inputs, lengths, slot_routes_all))
    return outputs.reshape(SLOTS * SLOT, D)

def reference(layer_input, attention_gain, query_weight, key_weight, value_weight, output_weight, expert_gain, router_weight, gate_weight, up_weight, down_weight, lengths, routes, cotangent):
    inputs_f = layer_input.astype(jnp.float32)
    weights = (attention_gain.astype(jnp.float32), query_weight.astype(jnp.float32), key_weight.astype(jnp.float32), value_weight.astype(jnp.float32), output_weight.astype(jnp.float32), expert_gain.astype(jnp.float32), router_weight.astype(jnp.float32), gate_weight.astype(jnp.float32), up_weight.astype(jnp.float32), down_weight.astype(jnp.float32))

    def forward(inputs_now, weights_now):
        return layer(inputs_now, weights_now, lengths, routes)
    output, pullback = jax.vjp(forward, inputs_f, weights)
    places = jnp.arange(SLOT, dtype=jnp.int32)
    valid = (places[None, :] < lengths[:, None]).reshape(SLOTS * SLOT, 1)
    slope = jnp.where(valid, cotangent.astype(jnp.float32), 0.0)
    input_slope, weight_slopes = pullback(slope)
    return (output.astype(jnp.bfloat16), input_slope.astype(jnp.bfloat16), weight_slopes[0], weight_slopes[1], weight_slopes[2], weight_slopes[3], weight_slopes[4], weight_slopes[5], weight_slopes[6], weight_slopes[7], weight_slopes[8], weight_slopes[9])
```

```python
import functools

import jax
import jax.numpy as jnp
import numpy as np
from jax import lax
from jax.experimental import pallas as pl
from jax.experimental.pallas import tpu as pltpu
from jax.sharding import PartitionSpec as P

D = 1024
HEADS = 16
KV = 8
HD = 64
EXPERTS = 32
TOP = 8
CAP = 288
ABSENT = -100000


epsilon = 1e-06
masked_score = -1e30
rotary_base = 10000.0


def chip_cycle(count):
    if count % 4 == 0 and count >= 8:
        wide = count // 4
        tall = 4
    else:
        return list(range(count))
    if wide == 1:
        return list(range(count))
    order = [row * wide for row in range(tall)]
    for step, row in enumerate(reversed(range(tall))):
        columns = range(1, wide) if step % 2 == 0 else reversed(range(1, wide))
        order += [row * wide + column for column in columns]
    return order


class Ring:
    def __init__(self, shards):
        chips = chip_cycle(shards // 2)
        count = len(chips)
        self.steps = count
        self.forward = []
        for place in range(count):
            here, there = chips[place], chips[(place + 1) % count]
            self.forward += [(2 * here, 2 * there), (2 * there + 1, 2 * here + 1)]
        self.swap = [(s, s ^ 1) for s in range(shards)]
        near = np.zeros((shards, count), np.int32)
        far = np.zeros((shards, count), np.int32)
        for place in range(count):
            for core in range(2):
                way = 1 - 2 * core
                for step in range(count):
                    me = 2 * chips[place] + core
                    near[me, step] = 2 * chips[(place - way * step) % count] + core
                    far[me, step] = 2 * chips[(place + way * step) % count] + 1 - core
        self.near, self.far = near, far

    def hop(self, array):
        return lax.ppermute(array, "shard", self.forward)

    def cross(self, array):
        return lax.ppermute(array, "shard", self.swap)

    def gather(self, array):
        near, far = [array], [self.cross(array)]
        for _ in range(self.steps - 1):
            near.append(self.hop(near[-1]))
            far.append(self.cross(near[-1]))
        return near, far


def rope_tables(length_rows, head_width):
    halfway = head_width // 2
    index_float = jnp.arange(halfway, dtype=jnp.float32)
    frequency = jnp.exp(-jnp.log(rotary_base) * index_float * 2.0 / head_width)
    angle = jnp.arange(length_rows, dtype=jnp.float32)[:, None] * frequency[None, :]
    return (jnp.cos(angle)[:, None, :], jnp.sin(angle)[:, None, :])


def rotate(values, cosine, sine):
    halfway = values.shape[-1] // 2
    first_half = values[..., :halfway]
    second_half = values[..., halfway:]
    return jnp.concatenate(
        [first_half * cosine - second_half * sine, second_half * cosine + first_half * sine],
        axis=-1,
    )


def unrotate(slopes, cosine, sine):
    halfway = slopes.shape[-1] // 2
    first_half = slopes[..., :halfway]
    second_half = slopes[..., halfway:]
    return jnp.concatenate(
        [first_half * cosine + second_half * sine, second_half * cosine - first_half * sine],
        axis=-1,
    )


def block_scores(query_block, keys, start_row, length, scale):
    products = (
        jnp.einsum("qhgd,khd->hgqk", query_block, keys, preferred_element_type=jnp.float32) * scale
    )
    query_place = start_row + jnp.arange(query_block.shape[0], dtype=jnp.int32)
    key_place = jnp.arange(keys.shape[0], dtype=jnp.int32)
    allowed = (key_place[None, :] <= query_place[:, None]) & (key_place[None, :] < length)
    return jnp.where(allowed[None, None], products, masked_score)


def dot(left, right):
    return jnp.dot(left, right, preferred_element_type=jnp.float32)


def experts_kernel(
    local_experts,
    chained,
    where_ref,
    tokens_ref,
    slope_ref,
    slot_row_ref,
    slot_column_ref,
    mask_ref,
    router_ref,
    in_ref,
    in_turned_ref,
    down_ref,
    down_turned_ref,
    *rest,
):
    rest = rest[5:] if chained else rest
    (
        back_ref,
        mix_ref,
        rows_ref,
        routed_ref,
        hidden_ref,
        slopes_ref,
        gate_slope_ref,
        mixed_rows,
        back_rows,
    ) = rest
    expert = pl.program_id(0)
    tokens = tokens_ref.shape[0]
    half = hidden_ref.shape[-1]
    bf16 = jnp.bfloat16

    slot_row = slot_row_ref[0, 0]
    place = lax.broadcasted_iota(jnp.int32, (CAP, tokens), 0)
    taken = slot_row == place
    pick = jnp.where(taken, 1.0, 0.0).astype(bf16)
    rows = dot(pick, tokens_ref[...]).astype(bf16)
    slope_rows = dot(pick, slope_ref[...])
    chosen = dot(pick, mask_ref[0])
    logits = dot(rows, router_ref[...])
    kept = jnp.where(chosen > 0.5, logits, masked_score)
    top = jnp.max(kept, axis=-1, keepdims=True)
    powered = jnp.exp(kept - top) * chosen
    total = jnp.sum(powered, axis=-1, keepdims=True)
    lane = lax.broadcasted_iota(jnp.int32, powered.shape, 1)
    mine = lane == where_ref[1] * local_experts + expert
    gate = jnp.sum(jnp.where(mine, powered, 0.0), axis=-1, keepdims=True) / jnp.where(
        total > 0.0, total, 1.0
    )
    both = dot(rows, in_ref[0])
    gate_part, up_part = both[:, :half], both[:, half:]
    sigma = 1.0 / (1.0 + jnp.exp(-gate_part))
    silu = gate_part * sigma
    hidden = (silu * up_part).astype(bf16)
    out = dot(hidden, down_ref[0]).astype(bf16).astype(jnp.float32)
    gate_slope = jnp.sum(out * slope_rows, axis=-1, keepdims=True)
    gate_slope_ref[0, 0] = jnp.sum(jnp.where(taken, gate_slope, 0.0), axis=0, keepdims=True)
    routed = (gate * slope_rows).astype(bf16)
    hidden_slope = dot(routed, down_turned_ref[0])
    gate_back = (hidden_slope * up_part * sigma * (1.0 + gate_part * (1.0 - sigma))).astype(bf16)
    up_back = (hidden_slope * silu).astype(bf16)
    slopes = jnp.concatenate([gate_back, up_back], axis=-1)
    back = dot(slopes, in_turned_ref[0]).astype(bf16)
    start = pl.multiple_of(expert * CAP, CAP)
    mixed_rows[pl.ds(start, CAP), :] = (gate * out).astype(bf16)
    back_rows[pl.ds(start, CAP), :] = back
    rows_ref[0] = rows
    routed_ref[0] = routed
    hidden_ref[0] = hidden
    slopes_ref[0] = slopes

    @pl.when(expert == local_experts - 1)
    def _():
        column = lax.broadcasted_iota(jnp.int32, (tokens, local_experts * CAP), 1)
        spread = jnp.zeros(column.shape, jnp.float32)
        for e in range(local_experts):
            spread = jnp.where(column - e * CAP == slot_column_ref[0, :, e : e + 1], 1.0, spread)
        spread = spread.astype(bf16)
        back_ref[...] = dot(spread, back_rows[...]).astype(bf16)
        mix_ref[...] = dot(spread, mixed_rows[...]).astype(bf16)


def experts_block(where, tokens_block, slope_block, plan, weights, kept):
    slot_row, slot_column, mask = plan
    router, into, into_turned, down, down_turned = weights
    tokens, width = tokens_block.shape
    blocks = slot_row.shape[0]
    local_experts, half = down.shape[0], down.shape[1]
    bf16 = jnp.bfloat16
    chained = kept is not None
    once = pl.Buffered(1)
    any_spec = pl.BlockSpec(memory_space=pl.ANY)
    in_specs = [
        pl.BlockSpec((tokens, width), lambda e, w: (0, 0), pipeline_mode=once),
        pl.BlockSpec((tokens, width), lambda e, w: (0, 0), pipeline_mode=once),
        pl.BlockSpec((1, 1, 1, tokens), lambda e, w: (w[0], e, 0, 0)),
        pl.BlockSpec((1, tokens, local_experts), lambda e, w: (w[0], 0, 0), pipeline_mode=once),
        pl.BlockSpec((1, tokens, EXPERTS), lambda e, w: (w[0], 0, 0), pipeline_mode=once),
        pl.BlockSpec((width, EXPERTS), lambda e, w: (0, 0), pipeline_mode=once),
        pl.BlockSpec((1, width, 2 * half), lambda e, w: (e, 0, 0)),
        pl.BlockSpec((1, 2 * half, width), lambda e, w: (e, 0, 0)),
        pl.BlockSpec((1, half, width), lambda e, w: (e, 0, 0)),
        pl.BlockSpec((1, width, half), lambda e, w: (e, 0, 0)),
    ]
    shapes = [
        jax.ShapeDtypeStruct((tokens, width), bf16),
        jax.ShapeDtypeStruct((tokens, width), bf16),
        jax.ShapeDtypeStruct((local_experts, blocks * CAP, width), bf16),
        jax.ShapeDtypeStruct((local_experts, blocks * CAP, width), bf16),
        jax.ShapeDtypeStruct((local_experts, blocks * CAP, half), bf16),
        jax.ShapeDtypeStruct((local_experts, blocks * CAP, 2 * half), bf16),
        jax.ShapeDtypeStruct((blocks, local_experts, 1, tokens), jnp.float32),
    ]
    out_specs = [
        pl.BlockSpec((tokens, width), lambda e, w: (0, 0), pipeline_mode=once),
        pl.BlockSpec((tokens, width), lambda e, w: (0, 0), pipeline_mode=once),
        pl.BlockSpec((1, CAP, width), lambda e, w: (e, w[0], 0)),
        pl.BlockSpec((1, CAP, width), lambda e, w: (e, w[0], 0)),
        pl.BlockSpec((1, CAP, half), lambda e, w: (e, w[0], 0)),
        pl.BlockSpec((1, CAP, 2 * half), lambda e, w: (e, w[0], 0)),
        pl.BlockSpec((1, 1, 1, tokens), lambda e, w: (w[0], e, 0, 0)),
    ]
    operands = [
        tokens_block, slope_block, slot_row, slot_column, mask,
        router, into, into_turned, down, down_turned,
    ]
    aliases = {}
    if chained:
        first = 1 + len(operands)
        operands += list(kept)
        in_specs += [any_spec] * 5
        aliases = {first + place: 2 + place for place in range(5)}
    flops = local_experts * 2 * CAP * (2 * tokens * width + 6 * width * half + 2 * tokens * width)
    return pl.pallas_call(
        functools.partial(experts_kernel, local_experts, chained),
        out_shape=shapes,
        grid_spec=pltpu.PrefetchScalarGridSpec(
            num_scalar_prefetch=1,
            grid=(local_experts,),
            in_specs=in_specs,
            out_specs=out_specs,
            scratch_shapes=[
                pltpu.VMEM((local_experts * CAP, width), bf16),
                pltpu.VMEM((local_experts * CAP, width), bf16),
            ],
        ),
        input_output_aliases=aliases,
        compiler_params=pltpu.CompilerParams(vmem_limit_bytes=52 * 1024 * 1024),
        cost_estimate=pl.CostEstimate(
            flops=flops, bytes_accessed=20 * 1024 * 1024, transcendentals=0
        ),
    )(where, *operands)


def on_device(
    shards,
    reps,
    layer_input,
    attention_gain,
    query_weight,
    key_weight,
    value_weight,
    output_weight,
    expert_gain,
    router_weight,
    gate_weight,
    up_weight,
    down_weight,
    lengths,
    routes,
    cotangent,
):
    ring = Ring(shards)
    me = lax.axis_index("shard")
    tokens = layer_input.shape[0]
    local_experts = gate_weight.shape[0]
    groups = HEADS // KV
    scale = HD ** (-0.5)
    length = lengths[0]
    bf16 = jnp.bfloat16

    packed = jnp.concatenate([query_weight, key_weight, value_weight, output_weight], axis=1)
    packed_full = lax.all_gather(packed, "shard", axis=0, tiled=True)
    input_full = packed_full[:, : (HEADS + 2 * KV) * HD]
    output_full = packed_full[:, (HEADS + 2 * KV) * HD :]

    expert_ids = jnp.arange(EXPERTS, dtype=jnp.int32)
    picks = jnp.any(routes[:, None, :] == expert_ids[None, :, None], axis=-1)
    picks_turned = picks.T
    earlier = jnp.triu(jnp.ones((tokens, tokens), bf16), k=1)
    ranks = dot(picks_turned.astype(bf16), earlier).astype(jnp.int32)
    slots_home = jnp.where(picks_turned, ranks, ABSENT)
    slots_all = lax.all_gather(slots_home, "shard", axis=0, tiled=False)
    slots_mine = lax.dynamic_slice_in_dim(slots_all, me * local_experts, local_experts, axis=1)
    slot_row = slots_mine[:, :, None, :]
    slot_column = jnp.swapaxes(slots_mine, 1, 2)
    mask = jnp.swapaxes((slots_all >= 0).astype(bf16), 1, 2)
    plan = (slot_row, slot_column, mask)
    into = jnp.concatenate([gate_weight, up_weight], axis=-1)
    weights = (
        router_weight,
        into,
        jnp.swapaxes(into, 1, 2),
        down_weight,
        jnp.swapaxes(down_weight, 1, 2),
    )

    valid = (jnp.arange(tokens, dtype=jnp.int32) < length)[:, None]
    slope_low = jnp.where(valid, cotangent, jnp.zeros_like(cotangent))
    slope_low, packed_full, slots_all = lax.optimization_barrier(
        (slope_low, packed_full, slots_all)
    )
    slope_near, slope_far = ring.gather(slope_low)
    slope = slope_low.astype(jnp.float32)

    inputs_f = layer_input.astype(jnp.float32)
    first_scale = lax.rsqrt(jnp.mean(inputs_f * inputs_f, axis=-1, keepdims=True) + epsilon)
    base_one = inputs_f * first_scale
    normed_one = (base_one * attention_gain).astype(bf16)
    cosine, sine = rope_tables(tokens, HD)
    heads_pre = dot(normed_one, input_full)
    query_pre = heads_pre[:, : HEADS * HD]
    key_pre = heads_pre[:, HEADS * HD : (HEADS + KV) * HD]
    values = heads_pre[:, (HEADS + KV) * HD :].astype(bf16).reshape(tokens, KV, HD)
    queries = (
        rotate(query_pre.reshape(tokens, HEADS, HD), cosine, sine)
        .astype(bf16)
        .reshape(tokens, KV, groups, HD)
    )
    keys = rotate(key_pre.reshape(tokens, KV, HD), cosine, sine).astype(bf16)
    block = min(512, tokens)
    block_count = tokens // block
    mixed_parts = []
    log_totals = []
    for block_index in range(block_count):
        start_row = block_index * block
        scores = block_scores(
            queries[start_row : start_row + block], keys, start_row, length, scale
        )
        maximum = jnp.max(scores, axis=-1, keepdims=True)
        powered = jnp.exp(scores - maximum)
        total = jnp.sum(powered, axis=-1, keepdims=True)
        probs = (powered / total).astype(bf16)
        log_totals.append(maximum + jnp.log(total))
        mixed_parts.append(
            jnp.einsum("hgqk,khd->qhgd", probs, values, preferred_element_type=jnp.float32)
        )
    attended = jnp.concatenate(mixed_parts, axis=0).reshape(tokens, HEADS * HD).astype(bf16)
    residual = inputs_f + dot(attended, output_full)
    second_scale = lax.rsqrt(jnp.mean(residual * residual, axis=-1, keepdims=True) + epsilon)
    base_two = residual * second_scale
    normed_two = (base_two * expert_gain).astype(bf16)

    near, far = ring.gather(normed_two)
    near_table, far_table = jnp.asarray(ring.near)[me], jnp.asarray(ring.far)[me]
    kept = None
    back_near, back_far, mix_near, mix_far = [], [], [], []
    for step in range(ring.steps):
        for side in ("far", "near"):
            here = side == "near"
            table = near_table if here else far_table
            results = experts_block(
                jnp.stack([table[step], me]).astype(jnp.int32),
                near[step] if here else far[step],
                slope_near[step] if here else slope_far[step],
                plan,
                weights,
                kept,
            )
            kept = results[2:]
            (back_near if here else back_far).append(results[0])
            (mix_near if here else mix_far).append(results[1])

    def ring_sum(near_parts, far_parts, after=None):
        def chip_part(step, arrived):
            parts = near_parts[step].astype(jnp.float32) + ring.cross(far_parts[step]).astype(
                jnp.float32
            )
            return parts if arrived is None else parts + arrived.astype(jnp.float32)

        total = None
        for step in range(1, ring.steps):
            total = ring.hop(chip_part(step, total).astype(bf16))
        return chip_part(0, total)

    normed_slope = ring_sum(back_near, back_far)
    rows_all, routed_all, hidden_all, slopes_all, gate_slopes = kept
    half = down_weight.shape[1]
    in_grad = jnp.einsum("erd,erf->edf", rows_all, slopes_all, preferred_element_type=jnp.float32)
    down_grad = jnp.einsum(
        "erf,erd->efd", hidden_all, routed_all, preferred_element_type=jnp.float32
    )

    gate_slope = lax.all_to_all(
        gate_slopes.reshape(shards, local_experts, tokens),
        "shard",
        split_axis=0,
        concat_axis=0,
        tiled=True,
    ).reshape(EXPERTS, tokens)
    logits = lax.dot_general(
        router_weight, normed_two, (((0,), (1,)), ((), ())), preferred_element_type=jnp.float32
    )
    kept_logits = jnp.where(picks_turned, logits, masked_score)
    powered = jnp.where(
        picks_turned, jnp.exp(kept_logits - jnp.max(kept_logits, axis=0, keepdims=True)), 0.0
    )
    gates = powered / jnp.sum(powered, axis=0, keepdims=True)
    mean_slope = jnp.sum(gates * gate_slope, axis=0, keepdims=True)
    logit_slope = (gates * (gate_slope - mean_slope)).astype(bf16)
    router_grad = lax.dot_general(
        normed_two, logit_slope, (((0,), (1,)), ((), ())), preferred_element_type=jnp.float32
    )
    normed_slope = normed_slope + lax.dot_general(
        logit_slope, router_weight, (((0,), (1,)), ((), ())), preferred_element_type=jnp.float32
    )

    mix_near, mix_far, normed_slope = lax.optimization_barrier((mix_near, mix_far, normed_slope))
    layer_output = (residual + ring_sum(mix_near, mix_far)).astype(bf16)

    expert_gain_grad = jnp.sum(normed_slope * base_two, axis=0)
    scaled_two = normed_slope * expert_gain
    residual_slope = (
        slope
        + second_scale * scaled_two
        - base_two
        * second_scale
        * second_scale
        * jnp.mean(scaled_two * residual, axis=-1, keepdims=True)
    )
    branch_slope = residual_slope.astype(bf16)
    output_grad = jnp.einsum(
        "sc,sd->cd", attended, branch_slope, preferred_element_type=jnp.float32
    )
    attended_slope = (
        jnp.einsum("sd,cd->sc", branch_slope, output_full, preferred_element_type=jnp.float32)
        .astype(bf16)
        .reshape(tokens, KV, groups, HD)
    )
    query_parts = []
    key_total = jnp.zeros((tokens, KV, HD), jnp.float32)
    value_total = jnp.zeros((tokens, KV, HD), jnp.float32)
    for block_index in range(block_count):
        start_row = block_index * block
        query_block = queries[start_row : start_row + block]
        mixed_slope = attended_slope[start_row : start_row + block]
        scores = block_scores(query_block, keys, start_row, length, scale)
        weights_soft = jnp.exp(scores - log_totals[block_index])
        probs = weights_soft.astype(bf16)
        probs_slope = jnp.einsum(
            "qhgd,khd->hgqk", mixed_slope, values, preferred_element_type=jnp.float32
        )
        centre = jnp.sum(weights_soft * probs_slope, axis=-1, keepdims=True)
        score_slope = (weights_soft * (probs_slope - centre)).astype(bf16)
        query_parts.append(
            jnp.einsum("hgqk,khd->qhgd", score_slope, keys, preferred_element_type=jnp.float32)
            * scale
        )
        key_total = (
            key_total
            + jnp.einsum(
                "hgqk,qhgd->khd", score_slope, query_block, preferred_element_type=jnp.float32
            )
            * scale
        )
        value_total = value_total + jnp.einsum(
            "hgqk,qhgd->khd", probs, mixed_slope, preferred_element_type=jnp.float32
        )
    query_slope = jnp.concatenate(query_parts, axis=0).reshape(tokens, HEADS, HD)
    query_pre_slope = unrotate(query_slope, cosine, sine).reshape(tokens, HEADS * HD).astype(bf16)
    key_pre_slope = unrotate(key_total, cosine, sine).reshape(tokens, KV * HD).astype(bf16)
    value_pre_slope = value_total.reshape(tokens, KV * HD).astype(bf16)
    pre_slopes = jnp.concatenate([query_pre_slope, key_pre_slope, value_pre_slope], axis=1)
    input_grad = jnp.einsum("sd,sc->dc", normed_one, pre_slopes, preferred_element_type=jnp.float32)
    normed_one_slope = jnp.einsum(
        "sc,dc->sd", pre_slopes, input_full, preferred_element_type=jnp.float32
    )
    attention_gain_grad = jnp.sum(normed_one_slope * base_one, axis=0)
    scaled_one = normed_one_slope * attention_gain
    input_slope = (
        residual_slope
        + first_scale * scaled_one
        - base_one
        * first_scale
        * first_scale
        * jnp.mean(scaled_one * inputs_f, axis=-1, keepdims=True)
    )
    input_gradient = input_slope.astype(bf16)

    def rep_sum(*arrays):
        if reps != 2:
            return lax.psum(arrays, "rep")
        low = [array.astype(bf16) for array in arrays]
        other = [lax.ppermute(array, "rep", [(0, 1), (1, 0)]) for array in low]
        return tuple(
            a.astype(jnp.float32) + b.astype(jnp.float32) for a, b in zip(low, other, strict=True)
        )

    in_sum, down_sum = rep_sum(in_grad, down_grad)
    gate_sum, up_sum = in_sum[..., :half], in_sum[..., half:]
    early = lax.psum(
        (expert_gain_grad, router_grad), ("shard", "rep")
    )
    gain_sum = lax.psum(attention_gain_grad, ("shard", "rep"))
    output_sum = lax.psum(
        lax.psum_scatter(output_grad, "shard", scatter_dimension=0, tiled=True), "rep"
    )
    input_sum = lax.psum(
        lax.psum_scatter(input_grad, "shard", scatter_dimension=0, tiled=True), "rep"
    )
    return (
        layer_output,
        input_gradient,
        gain_sum,
        input_sum[:, : HEADS * HD],
        input_sum[:, HEADS * HD : (HEADS + KV) * HD],
        input_sum[:, (HEADS + KV) * HD :],
        output_sum,
        early[0],
        early[1],
        gate_sum,
        up_sum,
        down_sum,
    )


def solution(mesh):
    return jax.shard_map(
        functools.partial(on_device, mesh.shape["shard"], mesh.shape["rep"]),
        mesh=mesh,
        in_specs=(
            P(("shard", "rep"), None),
            P(),
            P("shard", None),
            P("shard", None),
            P("shard", None),
            P("shard", None),
            P(),
            P(),
            P("shard", None, None),
            P("shard", None, None),
            P("shard", None, None),
            P(("shard", "rep")),
            P(("shard", "rep"), None),
            P(("shard", "rep"), None),
        ),
        out_specs=(
            P(("shard", "rep"), None),
            P(("shard", "rep"), None),
            P(),
            P("shard", None),
            P("shard", None),
            P("shard", None),
            P("shard", None),
            P(),
            P(),
            P("shard", None, None),
            P("shard", None, None),
            P("shard", None, None),
        ),
        check_vma=False,
    )
```

```python
import functools

import jax
import jax.numpy as jnp
import numpy as np
from jax import lax
from jax.experimental import pallas as pl
from jax.experimental.pallas import tpu as pltpu
from jax.sharding import PartitionSpec as P

D = 1024
HEADS = 16
KV = 8
HD = 64
EXPERTS = 32
TOP = 8
CAP = 288
ABSENT = -100000


epsilon = 1e-06
masked_score = -1e30
rotary_base = 10000.0


def chip_cycle(count):
    if count % 4 == 0 and count >= 8:
        wide = count // 4
        tall = 4
    else:
        return list(range(count))
    if wide == 1:
        return list(range(count))
    order = [row * wide for row in range(tall)]
    for step, row in enumerate(reversed(range(tall))):
        columns = range(1, wide) if step % 2 == 0 else reversed(range(1, wide))
        order += [row * wide + column for column in columns]
    return order


class Ring:
    def __init__(self, shards):
        chips = chip_cycle(shards // 2)
        count = len(chips)
        self.steps = count
        self.forward = []
        for place in range(count):
            here, there = chips[place], chips[(place + 1) % count]
            self.forward += [(2 * here, 2 * there), (2 * there + 1, 2 * here + 1)]
        self.swap = [(s, s ^ 1) for s in range(shards)]
        near = np.zeros((shards, count), np.int32)
        far = np.zeros((shards, count), np.int32)
        for place in range(count):
            for core in range(2):
                way = 1 - 2 * core
                for step in range(count):
                    me = 2 * chips[place] + core
                    near[me, step] = 2 * chips[(place - way * step) % count] + core
                    far[me, step] = 2 * chips[(place + way * step) % count] + 1 - core
        self.near, self.far = near, far

    def hop(self, array):
        return lax.ppermute(array, "shard", self.forward)

    def cross(self, array):
        return lax.ppermute(array, "shard", self.swap)

    def part_sum(self, near, far):
        return near.astype(jnp.float32) + self.cross(far).astype(jnp.float32)

    def scatter_sum(self, array, me):
        rows, columns = array.shape
        count = self.steps
        blocks = array.reshape(count, 2, rows // (2 * count), columns)
        core = lax.rem(me, 2)
        mine = lax.dynamic_index_in_dim(blocks, core, axis=1, keepdims=False)
        other = lax.dynamic_index_in_dim(blocks, 1 - core, axis=1, keepdims=False)
        parts = self.part_sum(mine, other.astype(jnp.bfloat16))
        chips = jnp.asarray(self.near // 2)[me]

        def part(step):
            return lax.dynamic_index_in_dim(parts, chips[step], axis=0, keepdims=False)

        total = None
        for step in range(1, count):
            here = part(step) if total is None else part(step) + total.astype(jnp.float32)
            total = self.hop(here.astype(jnp.bfloat16))
        return part(0) + total.astype(jnp.float32)

    def gather(self, array):
        near, far = [array], [self.cross(array)]
        for _ in range(self.steps - 1):
            near.append(self.hop(near[-1]))
            far.append(self.cross(near[-1]))
        return near, far


def rope_tables(tokens):
    halfway = HD // 2
    index_float = jnp.arange(halfway, dtype=jnp.float32)
    frequency = jnp.exp(-jnp.log(rotary_base) * index_float * 2.0 / HD)
    angle = jnp.arange(tokens, dtype=jnp.float32)[:, None] * frequency[None, :]
    cosine, sine = jnp.cos(angle), jnp.sin(angle)
    return (
        jnp.concatenate([cosine] * 4, axis=1),
        jnp.concatenate([-sine, sine, -sine, sine], axis=1),
    )


def dot(l,r): return jnp.dot(l,r,preferred_element_type=jnp.float32)
def dot_nt(l,r): return lax.dot_general(l,r,(((1,),(1,)),((),())),preferred_element_type=jnp.float32)
def dot_tn(l,r): return lax.dot_general(l,r,(((0,),(0,)),((),())),preferred_element_type=jnp.float32)

def swap_halves(values):
    parts=[]
    for start in range(0, values.shape[1], 128):
        part=values[:,start:start+128]
        lane=lax.broadcasted_iota(jnp.int32,part.shape,1)
        parts.append(jnp.where(lane % HD < HD//2, pltpu.roll(part,128-HD//2,1), pltpu.roll(part,HD//2,1)))
    return parts[0] if len(parts)==1 else jnp.concatenate(parts,axis=1)

def tile(table,width):
    return table if width==128 else jnp.concatenate([table]*(width//128),axis=1)

def forward_kernel(block, length_ref, normed_ref, wq_ref, wk_ref, wv_ref, cos_ref, sin_ref,
                   q_ref,k_ref,v_ref,out_ref,total_ref):
    tokens=normed_ref.shape[0]
    length=length_ref[0]
    cos,sin=cos_ref[...],sin_ref[...]
    bf16=jnp.bfloat16
    x=normed_ref[...]
    q=dot(x,wq_ref[...])
    q=q*tile(cos,q.shape[1])+swap_halves(q)*tile(sin,q.shape[1])
    q_ref[...]=(q.astype(bf16).astype(jnp.float32)*(HD**-0.5)).astype(bf16)
    k=dot(x,wk_ref[...])
    k_ref[...]=(k*cos+swap_halves(k)*sin).astype(bf16)
    v_ref[...]=dot(x,wv_ref[...]).astype(bf16)
    groups=HEADS//KV
    for head in range(2):
        for i in range(tokens//block):
            rows=slice(i*block,(i+1)*block)
            span=(i+1)*block
            keys=k_ref[:span,head*HD:(head+1)*HD]
            vals=v_ref[:span,head*HD:(head+1)*HD]
            qs=jnp.concatenate([q_ref[rows,(head*groups+h)*HD:(head*groups+h+1)*HD] for h in range(groups)],axis=0)
            s=dot_nt(keys,qs)
            key_place=lax.broadcasted_iota(jnp.int32,s.shape,0)
            query_place=lax.broadcasted_iota(jnp.int32,s.shape,1) % block + i*block
            s=jnp.where(key_place<=jnp.minimum(query_place,length-1),s,masked_score)
            top=jnp.max(s,axis=0,keepdims=True)
            p=jnp.exp(s-top)
            total=jnp.sum(p,axis=0,keepdims=True)
            p=(p*(1.0/total)).astype(bf16)
            o=dot_tn(p,vals)
            log_total=top+jnp.log(total)
            for h in range(groups):
                at=head*groups+h
                out_ref[rows,at*HD:(at+1)*HD]=o[h*block:(h+1)*block].astype(bf16)
                total_ref[0,at:at+1,rows]=log_total[:,h*block:(h+1)*block]

def attention_forward(length, normed, packed, cos, sin, part, block=256):
    tokens,width=normed.shape
    qw=HEADS*HD//4; kw=KV*HD//4
    bf16=jnp.bfloat16
    qb=HEADS*HD//kw; vb=(HEADS+KV)*HD//kw
    return pl.pallas_call(
        functools.partial(forward_kernel,block),
        out_shape=[jax.ShapeDtypeStruct((tokens,2*qw),bf16),jax.ShapeDtypeStruct((tokens,2*kw),bf16),jax.ShapeDtypeStruct((tokens,2*kw),bf16),
                   jax.ShapeDtypeStruct((tokens,2*qw),bf16),jax.ShapeDtypeStruct((2,HEADS//4,tokens),jnp.float32)],
        grid_spec=pltpu.PrefetchScalarGridSpec(num_scalar_prefetch=1,grid=(2,),
            in_specs=[pl.BlockSpec((tokens,width),lambda g,l:(0,0)),
                      pl.BlockSpec((width,qw),lambda g,l:(0,g+2*part)),
                      pl.BlockSpec((width,kw),lambda g,l:(0,qb+g+2*part)),
                      pl.BlockSpec((width,kw),lambda g,l:(0,vb+g+2*part)),
                      pl.BlockSpec((tokens,128),lambda g,l:(0,0)),pl.BlockSpec((tokens,128),lambda g,l:(0,0))],
            out_specs=[pl.BlockSpec((tokens,qw),lambda g,l:(0,g)),pl.BlockSpec((tokens,kw),lambda g,l:(0,g)),pl.BlockSpec((tokens,kw),lambda g,l:(0,g)),
                       pl.BlockSpec((tokens,qw),lambda g,l:(0,g)),pl.BlockSpec((1,HEADS//4,tokens),lambda g,l:(g,0,0))]),
        compiler_params=pltpu.CompilerParams(vmem_limit_bytes=40*1024*1024),
        cost_estimate=pl.CostEstimate(flops=30*10**9,bytes_accessed=20*1024*1024,transcendentals=0),
    )(length,normed,packed,packed,packed,cos,sin)

def backward_kernel(block,length_ref,q_ref,k_ref,v_ref,slope_ref,total_ref,cos_ref,sin_ref,dq_ref,dk_ref,dv_ref,dq_s,dk_s,dv_s):
    tokens=q_ref.shape[0]
    length=length_ref[0]
    bf16=jnp.bfloat16
    groups=HEADS//KV
    for head in range(2):
        lanes=slice(head*HD,(head+1)*HD)
        for i in reversed(range(tokens//block)):
            rows=slice(i*block,(i+1)*block)
            span=(i+1)*block
            keys=k_ref[:span,lanes]; vals=v_ref[:span,lanes]
            heads=[slice((head*groups+h)*HD,(head*groups+h+1)*HD) for h in range(groups)]
            qs=jnp.concatenate([q_ref[rows,at] for at in heads],axis=0)
            slopes=jnp.concatenate([slope_ref[rows,at] for at in heads],axis=0)
            log_total=jnp.concatenate([total_ref[0,head*groups+h:head*groups+h+1,rows] for h in range(groups)],axis=1)
            s=dot_nt(keys,qs)
            key_place=lax.broadcasted_iota(jnp.int32,s.shape,0)
            query_place=lax.broadcasted_iota(jnp.int32,s.shape,1) % block + i*block
            s=jnp.where(key_place<=jnp.minimum(query_place,length-1),s,masked_score)
            w=jnp.exp(s-log_total)
            ps=dot_nt(vals,slopes)
            centre=jnp.sum(w*ps,axis=0,keepdims=True)
            ds=(w*(ps-centre)).astype(bf16)
            dq=dot_tn(ds,keys)
            dk=dot(ds,qs)
            dv=dot(w.astype(bf16),slopes)
            for h in range(groups):
                dq_s[rows,heads[h]]=dq[h*block:(h+1)*block]*(HD**-0.5)
            if i==tokens//block-1:
                dk_s[:,lanes]=dk; dv_s[:,lanes]=dv
            else:
                dk_s[:span,lanes]+=dk; dv_s[:span,lanes]+=dv
    cos,sin=cos_ref[...],sin_ref[...]
    dq=dq_s[...]
    dq_ref[...]=(dq*tile(cos,dq.shape[1])-swap_halves(dq)*tile(sin,dq.shape[1])).astype(bf16)
    dk=dk_s[...]
    dk_ref[...]=(dk*cos-swap_halves(dk)*sin).astype(bf16)
    dv_ref[...]=dv_s[...].astype(bf16)

def attention_backward(length,q,k,v,slope,total,cos,sin,part,block=256):
    tokens=q.shape[0]
    qw=HEADS*HD//4; kw=KV*HD//4
    bf16=jnp.bfloat16
    qs=pl.BlockSpec((tokens,qw),lambda g,l:(0,g)); ks=pl.BlockSpec((tokens,kw),lambda g,l:(0,g)); cs=pl.BlockSpec((tokens,128),lambda g,l:(0,0))
    return pl.pallas_call(
        functools.partial(backward_kernel,block),
        out_shape=[jax.ShapeDtypeStruct((tokens,2*qw),bf16),jax.ShapeDtypeStruct((tokens,2*kw),bf16),jax.ShapeDtypeStruct((tokens,2*kw),bf16)],
        grid_spec=pltpu.PrefetchScalarGridSpec(num_scalar_prefetch=1,grid=(2,),
            in_specs=[qs,ks,ks,pl.BlockSpec((tokens,qw),lambda g,l:(0,g+2*part)),pl.BlockSpec((1,HEADS//4,tokens),lambda g,l:(g,0,0)),cs,cs],
            out_specs=[qs,ks,ks],
            scratch_shapes=[pltpu.VMEM((tokens,qw),jnp.float32),pltpu.VMEM((tokens,kw),jnp.float32),pltpu.VMEM((tokens,kw),jnp.float32)]),
        compiler_params=pltpu.CompilerParams(vmem_limit_bytes=40*1024*1024),
        cost_estimate=pl.CostEstimate(flops=20*10**9,bytes_accessed=10*1024*1024,transcendentals=0),
    )(length,q,k,v,slope,total,cos,sin)

def pair_kernel(local_experts, chained, where_ref, tokens_a, tokens_b, slope_a, slope_b, row_a, row_b, mask_a, mask_b,
                router_ref, gate_ref, up_ref, down_ref, *rest):
    rest = rest[4:] if chained else rest
    (back_a, back_b, mix_a, mix_b, rows_ref, routed_ref, hidden_ref, slopes_ref, gate_slope_ref, mixed_rows, back_rows, raw_slopes) = rest
    expert = pl.program_id(0)
    tokens = tokens_a.shape[0]
    half = hidden_ref.shape[-1]
    bf16 = jnp.bfloat16
    sides = ((tokens_a, slope_a, row_a, mask_a), (tokens_b, slope_b, row_b, mask_b))
    taken, chosen = [], []
    for side, (tokens_ref, slope_ref, row_ref, mask_ref) in enumerate(sides):
        place = lax.broadcasted_iota(jnp.int32, (CAP, tokens), 0)
        hit = row_ref[0, pl.ds(expert, 1)] == place
        taken.append(hit)
        pick = jnp.where(hit, 1.0, 0.0).astype(bf16)
        rows_ref[0, side * CAP : (side + 1) * CAP] = dot(pick, tokens_ref[...]).astype(bf16)
        raw_slopes[side * CAP : (side + 1) * CAP] = dot(pick, slope_ref[...]).astype(bf16)
        chosen.append(dot_nt(pick, mask_ref[0]))
    rows = rows_ref[0]
    chosen = jnp.concatenate(chosen, axis=0)
    logits = dot(rows, router_ref[...])
    kept = jnp.where(chosen > 0.5, logits, masked_score)
    top = jnp.max(kept, axis=-1, keepdims=True)
    powered = jnp.exp(kept - top) * chosen
    total = jnp.sum(powered, axis=-1, keepdims=True)
    lane = lax.broadcasted_iota(jnp.int32, powered.shape, 1)
    mine = lane == where_ref[2] * local_experts + expert
    gate = jnp.sum(jnp.where(mine, powered, 0.0), axis=-1, keepdims=True) / jnp.where(total > 0.0, total, 1.0)
    gate_part = dot(rows, gate_ref[0])
    up_part = dot(rows, up_ref[0])
    sigma = 1.0 / (1.0 + jnp.exp(-gate_part))
    silu = gate_part * sigma
    hidden = (silu * up_part).astype(bf16)
    hidden_ref[0] = hidden
    slope_rows = raw_slopes[...].astype(jnp.float32)
    routed = (gate * slope_rows).astype(bf16)
    routed_ref[0] = routed
    out = dot(hidden, down_ref[0]).astype(bf16).astype(jnp.float32)
    gate_slope = jnp.sum(out * slope_rows, axis=-1, keepdims=True)
    for side in range(2):
        part = gate_slope[side * CAP : (side + 1) * CAP]
        gate_slope_ref[side, 0] = jnp.sum(jnp.where(taken[side], part, 0.0), axis=0, keepdims=True)
    mixed = (gate * out).astype(bf16)
    hidden_slope = dot_nt(routed, down_ref[0])
    gate_back = (hidden_slope * up_part * sigma * (1.0 + gate_part * (1.0 - sigma))).astype(bf16)
    up_back = (hidden_slope * silu).astype(bf16)
    slopes_ref[0, :, :half] = gate_back
    slopes_ref[0, :, half:] = up_back
    back = (dot_nt(gate_back, gate_ref[0]) + dot_nt(up_back, up_ref[0])).astype(bf16)
    start = pl.multiple_of(expert * CAP, CAP)
    for side in range(2):
        mixed_rows[side, pl.ds(start, CAP), :] = mixed[side * CAP : (side + 1) * CAP]
        back_rows[side, pl.ds(start, CAP), :] = back[side * CAP : (side + 1) * CAP]

    @pl.when(expert == local_experts - 1)
    def _():
        for side, (column_ref, back_ref, mix_ref) in enumerate(((row_a, back_a, mix_a), (row_b, back_b, mix_b))):
            column = lax.broadcasted_iota(jnp.int32, (tokens, local_experts * CAP), 1)
            slots = jnp.transpose(column_ref[0])
            spread = jnp.zeros(column.shape, jnp.float32)
            for e in range(local_experts):
                spread = jnp.where(column - e * CAP == slots[:, e : e + 1], 1.0, spread)
            spread = spread.astype(bf16)
            back_ref[...] = dot(spread, back_rows[side]).astype(bf16)
            mix_ref[...] = dot(spread, mixed_rows[side]).astype(bf16)

def experts_pair(step, steps, where, ta, tb, sa, sb, plan, weights, kept):
    slot_row, mask = plan
    router, gate, up, down = weights
    tokens, width = ta.shape
    local_experts, half = down.shape[0], down.shape[1]
    bf16 = jnp.bfloat16
    chained = kept is not None
    once = pl.Buffered(1)
    block = lambda: pl.BlockSpec((tokens, width), lambda e, w: (0, 0), pipeline_mode=once)
    in_specs = [block(), block(), block(), block()]
    in_specs += [pl.BlockSpec((1, local_experts, tokens), lambda e, w, i=i: (w[i], 0, 0), pipeline_mode=once) for i in range(2)]
    in_specs += [pl.BlockSpec((1, EXPERTS, tokens), lambda e, w, i=i: (w[i], 0, 0), pipeline_mode=once) for i in range(2)]
    in_specs += [
        pl.BlockSpec((width, EXPERTS), lambda e, w: (0, 0), pipeline_mode=once),
        pl.BlockSpec((1, width, half), lambda e, w: (e, 0, 0)),
        pl.BlockSpec((1, width, half), lambda e, w: (e, 0, 0)),
        pl.BlockSpec((1, half, width), lambda e, w: (e, 0, 0)),
    ]
    S = jax.ShapeDtypeStruct
    R = 2 * CAP
    shapes = [S((tokens, width), bf16)] * 4 + [
        S((local_experts, steps * R, width), bf16), S((local_experts, steps * R, width), bf16),
        S((local_experts, steps * R, half), bf16), S((local_experts, steps * R, 2 * half), bf16),
        S((2, local_experts, 1, tokens), jnp.float32)]
    out_specs = [block(), block(), block(), block(),
        pl.BlockSpec((1, R, width), lambda e, w: (e, step, 0)),
        pl.BlockSpec((1, R, width), lambda e, w: (e, step, 0)),
        pl.BlockSpec((1, R, half), lambda e, w: (e, step, 0)),
        pl.BlockSpec((1, R, 2 * half), lambda e, w: (e, step, 0)),
        pl.BlockSpec((2, 1, 1, tokens), lambda e, w: (0, e, 0, 0))]
    operands = [ta, tb, sa, sb, slot_row, slot_row, mask, mask, router, gate, up, down]
    aliases = {}
    if chained:
        first = 1 + len(operands)
        operands += list(kept)
        in_specs += [pl.BlockSpec(memory_space=pl.ANY)] * 4
        aliases = {first + p: 4 + p for p in range(4)}
    flops = local_experts * 4 * CAP * (2 * tokens * width + 6 * width * half + 2 * tokens * width)
    return pl.pallas_call(
        functools.partial(pair_kernel, local_experts, chained),
        out_shape=shapes,
        grid_spec=pltpu.PrefetchScalarGridSpec(num_scalar_prefetch=1, grid=(local_experts,), in_specs=in_specs, out_specs=out_specs,
            scratch_shapes=[pltpu.VMEM((2, local_experts * CAP, width), bf16), pltpu.VMEM((2, local_experts * CAP, width), bf16), pltpu.VMEM((R, width), bf16)]),
        input_output_aliases=aliases,
        compiler_params=pltpu.CompilerParams(vmem_limit_bytes=60 * 1024 * 1024),
        cost_estimate=pl.CostEstimate(flops=flops, bytes_accessed=40 * 1024 * 1024, transcendentals=0),
    )(where, *operands)


def on_device(
    shards,
    reps,
    layer_input,
    attention_gain,
    query_weight,
    key_weight,
    value_weight,
    output_weight,
    expert_gain,
    router_weight,
    gate_weight,
    up_weight,
    down_weight,
    lengths,
    routes,
    cotangent,
):
    ring = Ring(shards)
    me = lax.axis_index("shard")
    tokens = layer_input.shape[0]
    local_experts, half = down_weight.shape[0], down_weight.shape[1]
    length = lengths[0]
    bf16 = jnp.bfloat16
    heads_width = (HEADS + 2 * KV) * HD

    expert_ids = jnp.arange(EXPERTS, dtype=jnp.int32)
    routes_turned = routes.T
    picks = functools.reduce(
        jnp.logical_or, [routes_turned[k][None, :] == expert_ids[:, None] for k in range(TOP)]
    )
    weight_rows = query_weight.shape[0]
    packed = jnp.concatenate(
        [query_weight, key_weight, value_weight, picks.astype(bf16).reshape(weight_rows, -1)],
        axis=1,
    )
    packed_full = lax.all_gather(packed, "shard", axis=0, tiled=True)
    packed_full, output_weight = lax.optimization_barrier((packed_full, output_weight))
    output_full = lax.all_gather(output_weight, "shard", axis=0, tiled=True)
    input_full = packed_full[:, :heads_width]

    valid = (jnp.arange(tokens, dtype=jnp.int32) < length)[:, None]
    slope_low = jnp.where(valid, cotangent, jnp.zeros_like(cotangent))
    slope = slope_low.astype(jnp.float32)
    slope_near = [slope_low]
    for _ in range(2):
        slope_near.append(ring.hop(slope_near[-1]))

    inputs_f = layer_input.astype(jnp.float32)
    first_scale = lax.rsqrt(jnp.mean(inputs_f * inputs_f, axis=-1, keepdims=True) + epsilon)
    base_one = inputs_f * first_scale
    normed_one = (base_one * attention_gain).astype(bf16)
    cosine, sine = rope_tables(tokens)
    packed_full, slope_near[-1] = lax.optimization_barrier((packed_full, slope_near[-1]))
    heads = []
    for part in range(2):
        heads.append(
            attention_forward(lengths, normed_one, packed_full, cosine, sine, part)
        )
        slope_near.append(ring.hop(slope_near[-1]))
        heads[-1], slope_near[-1], packed_full = lax.optimization_barrier(
            (heads[-1], slope_near[-1], packed_full)
        )
    attended = jnp.concatenate([heads[part][3] for part in range(2)], axis=1)
    residual = inputs_f + dot(attended, output_full)
    second_scale = lax.rsqrt(jnp.mean(residual * residual, axis=-1, keepdims=True) + epsilon)
    base_two = residual * second_scale
    normed_two = (base_two * expert_gain).astype(bf16)

    mask_all = packed_full[:, heads_width:].reshape(shards, EXPERTS, tokens)
    mask_mine = lax.dynamic_slice_in_dim(mask_all, me * local_experts, local_experts, axis=1)
    earlier = jnp.triu(jnp.ones((tokens, tokens), bf16), k=1)
    ranks = dot(mask_mine.reshape(shards * local_experts, tokens), earlier).astype(jnp.int32)
    slot_row = jnp.where(mask_mine > 0, ranks.reshape(mask_mine.shape), ABSENT)
    plan = (slot_row, mask_all)

    near = [normed_two]
    near_table, far_table = jnp.asarray(ring.near)[me], jnp.asarray(ring.far)[me]
    weights = (router_weight, gate_weight, up_weight, down_weight)
    kept, gate_slopes, total = None, [], None
    mix_near, mix_far, back_home = [], [], None
    for step in range(ring.steps):
        if step + 1 < ring.steps:
            near.append(ring.hop(near[-1]))
        if step > 0 and len(slope_near) < ring.steps:
            slope_near.append(ring.hop(slope_near[-1]))
            if step + 1 < ring.steps:
                near[-1], slope_near[-1] = lax.optimization_barrier((near[-1], slope_near[-1]))
        results = experts_pair(
            step,
            ring.steps,
            jnp.stack([near_table[step], far_table[step], me]).astype(jnp.int32),
            near[step],
            ring.cross(near[step]),
            slope_near[step],
            ring.cross(slope_near[step]),
            plan,
            weights,
            kept,
        )
        kept = results[4:8]
        mix_near.append(results[2])
        mix_far.append(results[3])
        gate_slopes.append(results[8])
        part = ring.part_sum(results[0], results[1])
        if step == 0:
            back_home = part
        else:
            total = part if total is None else part + total.astype(jnp.float32)
            total = ring.hop(total.astype(bf16))
    rows_all, routed_all, hidden_all, slopes_all = kept
    in_grad = [
        lax.dot_general(
            rows_all[e], slopes_all[e], (((0,), (0,)), ((), ())), preferred_element_type=jnp.float32
        ).astype(bf16)
        for e in range(local_experts)
    ]

    places = np.zeros((shards, shards), np.int32)
    for step in range(ring.steps):
        for shard in range(shards):
            places[shard, ring.near[shard, step]] = 2 * step
            places[shard, ring.far[shard, step]] = 2 * step + 1
    gate_slopes = jnp.concatenate(gate_slopes, axis=0)[:, :, 0, :]
    gate_slopes = jnp.take(gate_slopes, jnp.asarray(places)[me], axis=0)
    gate_slope = lax.all_to_all(
        gate_slopes, "shard", split_axis=0, concat_axis=0, tiled=True
    ).reshape(EXPERTS, tokens)
    logits = lax.dot_general(
        router_weight, normed_two, (((0,), (1,)), ((), ())), preferred_element_type=jnp.float32
    )
    kept_logits = jnp.where(picks, logits, masked_score)
    powered = jnp.where(
        picks, jnp.exp(kept_logits - jnp.max(kept_logits, axis=0, keepdims=True)), 0.0
    )
    gates = powered / jnp.sum(powered, axis=0, keepdims=True)
    mean_slope = jnp.sum(gates * gate_slope, axis=0, keepdims=True)
    logit_slope = (gates * (gate_slope - mean_slope)).astype(bf16)
    router_grad = dot(logit_slope, normed_two)
    normed_slope = (
        back_home
        + total.astype(jnp.float32)
        + lax.dot_general(
            logit_slope, router_weight, (((0,), (1,)), ((), ())), preferred_element_type=jnp.float32
        )
    )
    normed_slope, in_grad, mix_near, mix_far = lax.optimization_barrier(
        (normed_slope, in_grad, mix_near, mix_far)
    )

    def across(array):
        return lax.ppermute(array, "rep", [(0, 1), (1, 0)])

    def mix_hop(step, total):
        part = ring.part_sum(mix_near[step], mix_far[step])
        if total is not None:
            part = part + total.astype(jnp.float32)
        return ring.hop(part.astype(bf16))

    pair = reps == 2
    in_other = [across(in_grad[0])] if pair else []
    mix = mix_hop(1, None)
    expert_gain_grad = jnp.sum(normed_slope * base_two, axis=0)
    scaled_two = normed_slope * expert_gain
    residual_slope = (
        slope
        + second_scale * scaled_two
        - base_two
        * second_scale
        * second_scale
        * jnp.mean(scaled_two * residual, axis=-1, keepdims=True)
    )
    branch_slope = residual_slope.astype(bf16)
    output_grad = lax.dot_general(
        attended, branch_slope, (((0,), (0,)), ((), ())), preferred_element_type=jnp.float32
    ).astype(bf16)
    attended_slope = jnp.einsum(
        "sd,cd->sc", branch_slope, output_full, preferred_element_type=jnp.float32
    ).astype(bf16)
    output_owned = lax.psum_scatter(output_grad, "shard", scatter_dimension=0, tiled=True)

    slopes_out = []
    mix_step = 2
    for part in range(2):
        attended_slope, mix = lax.optimization_barrier((attended_slope, mix))
        if mix_step < ring.steps:
            mix = mix_hop(mix_step, mix)
            mix_step += 1
        queries, keys, values, _, log_totals = heads[part]
        slopes_out.append(
            attention_backward(
                lengths, queries, keys, values, attended_slope, log_totals, cosine, sine, part
            )
        )
        if part == 0:
            attended_slope, slopes_out[0], in_other = lax.optimization_barrier(
                (attended_slope, slopes_out[0], in_other)
            )
            if pair and local_experts > 1:
                in_other.append(across(in_grad[1]))
    pre_slopes = jnp.concatenate(
        [slopes_out[part][which] for which in range(3) for part in range(2)], axis=1
    )
    pre_slopes, mix = lax.optimization_barrier((pre_slopes, mix))
    if mix_step < ring.steps:
        mix = mix_hop(mix_step, mix)
        mix_step += 1
    input_grad = lax.dot_general(
        normed_one, pre_slopes, (((0,), (0,)), ((), ())), preferred_element_type=jnp.float32
    ).astype(bf16)
    input_owned = lax.psum_scatter(input_grad, "shard", scatter_dimension=0, tiled=True)
    normed_one_slope = jnp.einsum(
        "sc,dc->sd", pre_slopes, input_full, preferred_element_type=jnp.float32
    )
    hidden_all, normed_one_slope = lax.optimization_barrier((hidden_all, normed_one_slope))
    down_grad = jnp.einsum(
        "erf,erd->efd", hidden_all, routed_all, preferred_element_type=jnp.float32
    ).astype(bf16)
    attention_gain_grad = jnp.sum(normed_one_slope * base_one, axis=0)
    scaled_one = normed_one_slope * attention_gain
    input_slope = (
        residual_slope
        + first_scale * scaled_one
        - base_one
        * first_scale
        * first_scale
        * jnp.mean(scaled_one * inputs_f, axis=-1, keepdims=True)
    )
    input_gradient = input_slope.astype(bf16)
    if pair:
        in_other, down_grad = lax.optimization_barrier((in_other, down_grad))
    mix, down_grad = lax.optimization_barrier((mix, down_grad))
    if pair:
        down_other = across(down_grad)
    while mix_step < ring.steps:
        mix = mix_hop(mix_step, mix)
        if pair and mix_step == ring.steps - 2:
            mix, down_other = lax.optimization_barrier((mix, down_other))
        mix_step += 1
    layer_output = (
        residual + ring.part_sum(mix_near[0], mix_far[0]) + mix.astype(jnp.float32)
    ).astype(bf16)

    def rep_sum(*arrays):
        if not pair:
            return lax.psum(tuple(array.astype(jnp.float32) for array in arrays), "rep")
        low = [array.astype(bf16) for array in arrays]
        return tuple(a.astype(jnp.float32) + across(a).astype(jnp.float32) for a in low)

    if pair:
        in_sum = jnp.stack(
            [a.astype(jnp.float32) + b.astype(jnp.float32) for a, b in zip(in_grad, in_other)]
        )
        down_sum = down_grad.astype(jnp.float32) + down_other.astype(jnp.float32)
    else:
        in_sum, down_sum = rep_sum(jnp.stack(in_grad), down_grad)
    gain_sum = jnp.concatenate(
        [attention_gain_grad[None], expert_gain_grad[None], router_grad], axis=0
    )
    for axis, size in (("rep", reps), ("shard", shards)):
        far_bit = 1
        while far_bit < size:
            gain_sum = gain_sum + lax.ppermute(
                gain_sum, axis, [(place, place ^ far_bit) for place in range(size)]
            )
            far_bit *= 2
    output_sum, input_sum = rep_sum(output_owned, input_owned)
    return (
        layer_output,
        input_gradient,
        gain_sum[0],
        input_sum[:, : HEADS * HD],
        input_sum[:, HEADS * HD : (HEADS + KV) * HD],
        input_sum[:, (HEADS + KV) * HD :],
        output_sum,
        gain_sum[1],
        gain_sum[2:].T,
        in_sum[..., :half],
        in_sum[..., half:],
        down_sum,
    )


def solution(mesh):
    return jax.shard_map(
        functools.partial(on_device, mesh.shape["shard"], mesh.shape["rep"]),
        mesh=mesh,
        in_specs=(
            P(("shard", "rep"), None),
            P(),
            P("shard", None),
            P("shard", None),
            P("shard", None),
            P("shard", None),
            P(),
            P(),
            P("shard", None, None),
            P("shard", None, None),
            P("shard", None, None),
            P(("shard", "rep")),
            P(("shard", "rep"), None),
            P(("shard", "rep"), None),
        ),
        out_specs=(
            P(("shard", "rep"), None),
            P(("shard", "rep"), None),
            P(),
            P("shard", None),
            P("shard", None),
            P("shard", None),
            P("shard", None),
            P(),
            P(),
            P("shard", None, None),
            P("shard", None, None),
            P("shard", None, None),
        ),
        check_vma=False,
    )
```

```python
import functools

import jax
import jax.numpy as jnp
import numpy as np
from jax import lax
from jax.experimental import pallas as pl
from jax.experimental.pallas import tpu as pltpu
from jax.sharding import PartitionSpec as P

D = 1024
HEADS = 16
KV = 8
HD = 64
EXPERTS = 32
TOP = 8
CAP = 288
ABSENT = -100000


epsilon = 1e-06
masked_score = -1e30
rotary_base = 10000.0


def chip_cycle(count):
    if count % 4 == 0 and count >= 8:
        wide = count // 4
        tall = 4
    else:
        return list(range(count))
    if wide == 1:
        return list(range(count))
    order = [row * wide for row in range(tall)]
    for step, row in enumerate(reversed(range(tall))):
        columns = range(1, wide) if step % 2 == 0 else reversed(range(1, wide))
        order += [row * wide + column for column in columns]
    return order


class Ring:
    def __init__(self, shards, reps, layers):
        if layers > 1:
            wide = shards // (2 * layers)
            cells = [
                [(layer * wide + x, y) for y in range(reps) for x in (range(wide) if y % 2 == 0 else reversed(range(wide)))]
                for layer in range(layers)
            ]
        else:
            cells = [[(chip, rep) for chip in chip_cycle(shards // 2)] for rep in range(reps)]
        self.steps = len(cells[0])
        self.forward, self.swap = [], []

        def device(chip, core):
            return (2 * chip[0] + core) * reps + chip[1]

        for cell in cells:
            for place, here in enumerate(cell):
                there = cell[(place + 1) % len(cell)]
                self.forward += [
                    (device(here, 0), device(there, 0)),
                    (device(there, 1), device(here, 1)),
                ]
                self.swap += [(device(here, 0), device(here, 1)), (device(here, 1), device(here, 0))]

    def hop(self, array):
        return lax.ppermute(array, ("shard", "rep"), self.forward)

    def cross(self, array):
        return lax.ppermute(array, ("shard", "rep"), self.swap)

    def part_sum(self, near, far, *more):
        far = far[0] if len(far) == 1 else sum(part.astype(jnp.float32) for part in far)
        parts = [*near, self.cross(far.astype(jnp.bfloat16)), *more]
        return sum(part.astype(jnp.float32) for part in parts)


def rope_tables(tokens):
    halfway = HD // 2
    index_float = jnp.arange(halfway, dtype=jnp.float32)
    frequency = jnp.exp(-jnp.log(rotary_base) * index_float * 2.0 / HD)
    angle = jnp.arange(tokens, dtype=jnp.float32)[:, None] * frequency[None, :]
    cosine, sine = jnp.cos(angle), jnp.sin(angle)
    return (
        jnp.concatenate([cosine] * 4, axis=1),
        jnp.concatenate([-sine, sine, -sine, sine], axis=1),
    )


def dot(l,r): return jnp.dot(l,r,preferred_element_type=jnp.float32)
def dot_nt(l,r): return lax.dot_general(l,r,(((1,),(1,)),((),())),preferred_element_type=jnp.float32)
def dot_tn(l,r): return lax.dot_general(l,r,(((0,),(0,)),((),())),preferred_element_type=jnp.float32)

def swap_halves(values):
    parts=[]
    for start in range(0, values.shape[1], 128):
        part=values[:,start:start+128]
        lane=lax.broadcasted_iota(jnp.int32,part.shape,1)
        parts.append(jnp.where(lane % HD < HD//2, pltpu.roll(part,128-HD//2,1), pltpu.roll(part,HD//2,1)))
    return parts[0] if len(parts)==1 else jnp.concatenate(parts,axis=1)

def tile(table,width):
    return table if width==128 else jnp.concatenate([table]*(width//128),axis=1)

def forward_kernel(block, length_ref, normed_ref, wq_ref, wk_ref, wv_ref, cos_ref, sin_ref,
                   q_ref,k_ref,v_ref,out_ref,total_ref):
    tokens=normed_ref.shape[0]
    length=length_ref[0]
    cos,sin=cos_ref[...],sin_ref[...]
    bf16=jnp.bfloat16
    x=normed_ref[...]
    q=dot(x,wq_ref[...])
    q=q*tile(cos,q.shape[1])+swap_halves(q)*tile(sin,q.shape[1])
    q_ref[...]=(q.astype(bf16).astype(jnp.float32)*(HD**-0.5)).astype(bf16)
    k=dot(x,wk_ref[...])
    k_ref[...]=(k*cos+swap_halves(k)*sin).astype(bf16)
    v_ref[...]=dot(x,wv_ref[...]).astype(bf16)
    groups=HEADS//KV
    for head in range(2):
        for i in range(tokens//block):
            rows=slice(i*block,(i+1)*block)
            span=(i+1)*block
            keys=k_ref[:span,head*HD:(head+1)*HD]
            vals=v_ref[:span,head*HD:(head+1)*HD]
            qs=jnp.concatenate([q_ref[rows,(head*groups+h)*HD:(head*groups+h+1)*HD] for h in range(groups)],axis=0)
            s=dot_nt(keys,qs)
            key_place=lax.broadcasted_iota(jnp.int32,s.shape,0)
            query_place=lax.broadcasted_iota(jnp.int32,s.shape,1) % block + i*block
            s=jnp.where(key_place<=jnp.minimum(query_place,length-1),s,masked_score)
            top=jnp.max(s,axis=0,keepdims=True)
            p=jnp.exp(s-top)
            total=jnp.sum(p,axis=0,keepdims=True)
            p=(p*(1.0/total)).astype(bf16)
            o=dot_tn(p,vals)
            log_total=top+jnp.log(total)
            for h in range(groups):
                at=head*groups+h
                out_ref[rows,at*HD:(at+1)*HD]=o[h*block:(h+1)*block].astype(bf16)
                total_ref[0,at:at+1,rows]=log_total[:,h*block:(h+1)*block]

def attention_forward(length, normed, packed, cos, sin, part, block=256):
    tokens,width=normed.shape
    qw=HEADS*HD//4; kw=KV*HD//4
    bf16=jnp.bfloat16
    qb=HEADS*HD//kw; vb=(HEADS+KV)*HD//kw
    return pl.pallas_call(
        functools.partial(forward_kernel,block),
        out_shape=[jax.ShapeDtypeStruct((tokens,2*qw),bf16),jax.ShapeDtypeStruct((tokens,2*kw),bf16),jax.ShapeDtypeStruct((tokens,2*kw),bf16),
                   jax.ShapeDtypeStruct((tokens,2*qw),bf16),jax.ShapeDtypeStruct((2,HEADS//4,tokens),jnp.float32)],
        grid_spec=pltpu.PrefetchScalarGridSpec(num_scalar_prefetch=1,grid=(2,),
            in_specs=[pl.BlockSpec((tokens,width),lambda g,l:(0,0)),
                      pl.BlockSpec((width,qw),lambda g,l:(0,g+2*part)),
                      pl.BlockSpec((width,kw),lambda g,l:(0,qb+g+2*part)),
                      pl.BlockSpec((width,kw),lambda g,l:(0,vb+g+2*part)),
                      pl.BlockSpec((tokens,128),lambda g,l:(0,0)),pl.BlockSpec((tokens,128),lambda g,l:(0,0))],
            out_specs=[pl.BlockSpec((tokens,qw),lambda g,l:(0,g)),pl.BlockSpec((tokens,kw),lambda g,l:(0,g)),pl.BlockSpec((tokens,kw),lambda g,l:(0,g)),
                       pl.BlockSpec((tokens,qw),lambda g,l:(0,g)),pl.BlockSpec((1,HEADS//4,tokens),lambda g,l:(g,0,0))]),
        compiler_params=pltpu.CompilerParams(vmem_limit_bytes=40*1024*1024),
        cost_estimate=pl.CostEstimate(flops=30*10**9,bytes_accessed=20*1024*1024,transcendentals=0),
    )(length,normed,packed,packed,packed,cos,sin)

def backward_kernel(block,length_ref,q_ref,k_ref,v_ref,slope_ref,total_ref,cos_ref,sin_ref,dq_ref,dk_ref,dv_ref,dq_s,dk_s,dv_s):
    tokens=q_ref.shape[0]
    length=length_ref[0]
    bf16=jnp.bfloat16
    groups=HEADS//KV
    for head in range(2):
        lanes=slice(head*HD,(head+1)*HD)
        for i in reversed(range(tokens//block)):
            rows=slice(i*block,(i+1)*block)
            span=(i+1)*block
            keys=k_ref[:span,lanes]; vals=v_ref[:span,lanes]
            heads=[slice((head*groups+h)*HD,(head*groups+h+1)*HD) for h in range(groups)]
            qs=jnp.concatenate([q_ref[rows,at] for at in heads],axis=0)
            slopes=jnp.concatenate([slope_ref[rows,at] for at in heads],axis=0)
            log_total=jnp.concatenate([total_ref[0,head*groups+h:head*groups+h+1,rows] for h in range(groups)],axis=1)
            s=dot_nt(keys,qs)
            key_place=lax.broadcasted_iota(jnp.int32,s.shape,0)
            query_place=lax.broadcasted_iota(jnp.int32,s.shape,1) % block + i*block
            s=jnp.where(key_place<=jnp.minimum(query_place,length-1),s,masked_score)
            w=jnp.exp(s-log_total)
            ps=dot_nt(vals,slopes)
            centre=jnp.sum(w*ps,axis=0,keepdims=True)
            ds=(w*(ps-centre)).astype(bf16)
            dq=dot_tn(ds,keys)
            dk=dot(ds,qs)
            dv=dot(w.astype(bf16),slopes)
            for h in range(groups):
                dq_s[rows,heads[h]]=dq[h*block:(h+1)*block]*(HD**-0.5)
            if i==tokens//block-1:
                dk_s[:,lanes]=dk; dv_s[:,lanes]=dv
            else:
                dk_s[:span,lanes]+=dk; dv_s[:span,lanes]+=dv
    cos,sin=cos_ref[...],sin_ref[...]
    dq=dq_s[...]
    dq_ref[...]=(dq*tile(cos,dq.shape[1])-swap_halves(dq)*tile(sin,dq.shape[1])).astype(bf16)
    dk=dk_s[...]
    dk_ref[...]=(dk*cos-swap_halves(dk)*sin).astype(bf16)
    dv_ref[...]=dv_s[...].astype(bf16)

def attention_backward(length,q,k,v,slope,total,cos,sin,part,block=256):
    tokens=q.shape[0]
    qw=HEADS*HD//4; kw=KV*HD//4
    bf16=jnp.bfloat16
    qs=pl.BlockSpec((tokens,qw),lambda g,l:(0,g)); ks=pl.BlockSpec((tokens,kw),lambda g,l:(0,g)); cs=pl.BlockSpec((tokens,128),lambda g,l:(0,0))
    return pl.pallas_call(
        functools.partial(backward_kernel,block),
        out_shape=[jax.ShapeDtypeStruct((tokens,2*qw),bf16),jax.ShapeDtypeStruct((tokens,2*kw),bf16),jax.ShapeDtypeStruct((tokens,2*kw),bf16)],
        grid_spec=pltpu.PrefetchScalarGridSpec(num_scalar_prefetch=1,grid=(2,),
            in_specs=[qs,ks,ks,pl.BlockSpec((tokens,qw),lambda g,l:(0,g+2*part)),pl.BlockSpec((1,HEADS//4,tokens),lambda g,l:(g,0,0)),cs,cs],
            out_specs=[qs,ks,ks],
            scratch_shapes=[pltpu.VMEM((tokens,qw),jnp.float32),pltpu.VMEM((tokens,kw),jnp.float32),pltpu.VMEM((tokens,kw),jnp.float32)]),
        compiler_params=pltpu.CompilerParams(vmem_limit_bytes=40*1024*1024),
        cost_estimate=pl.CostEstimate(flops=20*10**9,bytes_accessed=10*1024*1024,transcendentals=0),
    )(length,q,k,v,slope,total,cos,sin)

def pair_kernel(
    count,
    step,
    chained,
    ids_ref,
    tokens_a,
    tokens_b,
    slope_a,
    slope_b,
    row_a,
    row_b,
    mask_a,
    mask_b,
    router_ref,
    *rest,
):
    weights, rest = rest[: 3 * count], rest[3 * count :]
    rest = rest[4:] if chained else rest
    back_out, mix_out, kept_out, rest = rest[0:2], rest[2:4], rest[4:8], rest[8:]
    blocks, backs, mixes, gates_in, ups_in, downs_in, rest = *rest[:6], rest[6:]
    rows_buf, routed_buf, hidden_buf, slopes_buf, raw_buf, mixed_rows, back_rows, rest = (
        *rest[:7],
        rest[7:],
    )
    load_sems, weight_sems, back_sems, mix_sems, kept_sems = rest
    tokens = blocks.shape[1]
    pair_rows = 2 * CAP
    bf16, f32 = jnp.bfloat16, jnp.float32
    sources = (tokens_a, slope_a, tokens_b, slope_b)

    def load(which):
        return pltpu.make_async_copy(
            sources[which].at[pl.ds(0, tokens)], blocks.at[which], load_sems.at[which]
        )

    def load_weight(e, which):
        target = (gates_in, ups_in, downs_in)[which].at[e]
        return pltpu.make_async_copy(weights[3 * e + which], target, weight_sems.at[e, which])

    stores = []

    def store(source, target, sem):
        stores.append(pltpu.make_async_copy(source, target, sem))
        stores[-1].start()

    def keep(e, which):
        source = (rows_buf, routed_buf, hidden_buf, slopes_buf)[which].at[e]
        target = kept_out[which].at[e, pl.ds(step * pair_rows, pair_rows)]
        store(source, target, kept_sems.at[e, which])

    for which in (0, 2, 1, 3):
        load(which).start()
    for e in range(count):
        for which in range(3):
            load_weight(e, which).start()

    taken, picks, chosen = [], [], []
    for side, (row_ref, mask_ref) in enumerate(((row_a, mask_a), (row_b, mask_b))):
        place = lax.broadcasted_iota(jnp.int32, (CAP, tokens), 0)
        taken.append([row_ref[0, e : e + 1] == place for e in range(count)])
        hits = [jnp.where(hit, 1.0, 0.0).astype(bf16) for hit in taken[side]]
        picks.append(hits[0] if count == 1 else jnp.concatenate(hits, axis=0))
        chosen.append(dot_nt(picks[side], mask_ref[...]))
        load(2 * side).wait()
        rows = dot(picks[side], blocks[2 * side]).astype(bf16)
        for e in range(count):
            rows_buf[e, side * CAP : (side + 1) * CAP] = rows[e * CAP : (e + 1) * CAP]
    for e in range(count):
        keep(e, 0)
    for side in range(2):
        load(2 * side + 1).wait()
        rows = dot(picks[side], blocks[2 * side + 1]).astype(bf16)
        for e in range(count):
            raw_buf[e, side * CAP : (side + 1) * CAP] = rows[e * CAP : (e + 1) * CAP]
    homeward = [[], []]
    for e in range(count):
        rows = rows_buf[e]
        marks = jnp.concatenate([chosen[side][e * CAP : (e + 1) * CAP] for side in range(2)], axis=0)
        logits = dot(rows, router_ref[...])
        kept = jnp.where(marks > 0.5, logits, masked_score)
        top = jnp.max(kept, axis=-1, keepdims=True)
        powered = jnp.exp(kept - top) * marks
        total = jnp.sum(powered, axis=-1, keepdims=True)
        lane = lax.broadcasted_iota(jnp.int32, powered.shape, 1)
        mine = lane == ids_ref[e]
        gate = jnp.sum(jnp.where(mine, powered, 0.0), axis=-1, keepdims=True) / jnp.where(
            total > 0.0, total, 1.0
        )
        slope_rows = raw_buf[e].astype(f32)
        routed = (gate * slope_rows).astype(bf16)
        routed_buf[e] = routed
        keep(e, 1)
        for which in range(3):
            load_weight(e, which).wait()
        gate_part = dot(rows, gates_in[e])
        up_part = dot(rows, ups_in[e])
        hidden_slope = dot_nt(routed, downs_in[e])
        sigma = 1.0 / (1.0 + jnp.exp(-gate_part))
        silu = gate_part * sigma
        hidden = (silu * up_part).astype(bf16)
        hidden_buf[e] = hidden
        keep(e, 2)
        gate_back = (hidden_slope * up_part * sigma * (1.0 + gate_part * (1.0 - sigma))).astype(bf16)
        up_back = (hidden_slope * silu).astype(bf16)
        half = gate_back.shape[1]
        slopes_buf[e, :, :half] = gate_back
        slopes_buf[e, :, half:] = up_back
        keep(e, 3)
        out = dot(hidden, downs_in[e]).astype(bf16).astype(f32)
        back = (dot_nt(gate_back, gates_in[e]) + dot_nt(up_back, ups_in[e])).astype(bf16)
        gate_slope = jnp.sum(out * slope_rows, axis=-1, keepdims=True)
        mixed = (gate * out).astype(bf16)
        for side in range(2):
            part = slice(side * CAP, (side + 1) * CAP)
            homeward[side].append(
                jnp.sum(jnp.where(taken[side][e], gate_slope[part], 0.0), axis=0, keepdims=True)
            )
            mixed_rows[side, e * CAP : (e + 1) * CAP] = mixed[part]
            back_rows[side, e * CAP : (e + 1) * CAP] = back[part]
    for side, row_ref in enumerate((row_a, row_b)):
        backs[side, :tokens] = dot_tn(picks[side], back_rows[side]).astype(bf16)
        row = lax.broadcasted_iota(jnp.int32, (EXPERTS, tokens), 0)
        whole = jnp.zeros(row.shape, f32)
        for e in range(count):
            whole = jnp.where(row == ids_ref[e], homeward[side][e], whole)
        high = whole.astype(bf16)
        backs[side, tokens : tokens + EXPERTS] = high
        backs[side, tokens + EXPERTS :] = (whole - high.astype(f32)).astype(bf16)
        store(backs.at[side], back_out[side], back_sems.at[side])
        mixes[side] = dot_tn(picks[side], mixed_rows[side]).astype(bf16)
        store(mixes.at[side], mix_out[side], mix_sems.at[side])
    for copy in stores:
        copy.wait()


def experts_pair(step, steps, expert_ids, ta, tb, sa, sb, slots, weights, kept):
    router, *weights = weights
    tokens, width = ta.shape
    count, half = len(weights) // 3, weights[2].shape[0]
    bf16 = jnp.bfloat16
    chained = kept is not None
    once = pl.Buffered(1)
    back_rows = tokens + 2 * EXPERTS

    def block(rows, at=0):
        return pl.BlockSpec((rows, width), lambda e, w: (at, 0), pipeline_mode=once)

    anywhere = pl.BlockSpec(memory_space=pl.ANY)
    in_specs = [anywhere] * 4
    in_specs += [
        pl.BlockSpec((1, count, tokens), lambda e, w, i=i: (2 * step + i, 0, 0), pipeline_mode=once)
        for i in range(2)
    ]
    in_specs += [block(EXPERTS, tokens // EXPERTS)] * 2
    in_specs += [pl.BlockSpec((width, EXPERTS), lambda e, w: (0, 0), pipeline_mode=once)]
    in_specs += [anywhere] * len(weights)
    rows = 2 * CAP
    columns = (width, width, half, 2 * half)
    shapes = [jax.ShapeDtypeStruct((back_rows, width), bf16)] * 2
    shapes += [jax.ShapeDtypeStruct((tokens, width), bf16)] * 2
    shapes += [jax.ShapeDtypeStruct((count, steps * rows, column), bf16) for column in columns]
    out_specs = [anywhere] * 8
    operands = [ta, tb, sa, sb, slots, slots, sa, sb, router, *weights]
    aliases = {}
    if chained:
        first = 1 + len(operands)
        operands += list(kept)
        in_specs += [anywhere] * 4
        aliases = {first + p: 4 + p for p in range(4)}
    flops = count * 2 * rows * (4 * tokens * width + 6 * width * half)
    return pl.pallas_call(
        functools.partial(pair_kernel, count, step, chained),
        out_shape=shapes,
        grid_spec=pltpu.PrefetchScalarGridSpec(
            num_scalar_prefetch=1,
            grid=(1,),
            in_specs=in_specs,
            out_specs=out_specs,
            scratch_shapes=[
                pltpu.VMEM((4, tokens, width), bf16),
                pltpu.VMEM((2, back_rows, width), bf16),
                pltpu.VMEM((2, tokens, width), bf16),
                pltpu.VMEM((count, width, half), bf16),
                pltpu.VMEM((count, width, half), bf16),
                pltpu.VMEM((count, half, width), bf16),
                *[pltpu.VMEM((count, rows, column), bf16) for column in columns],
                pltpu.VMEM((count, rows, width), bf16),
                pltpu.VMEM((2, count * CAP, width), bf16),
                pltpu.VMEM((2, count * CAP, width), bf16),
                pltpu.SemaphoreType.DMA((4,)),
                pltpu.SemaphoreType.DMA((count, 3)),
                pltpu.SemaphoreType.DMA((2,)),
                pltpu.SemaphoreType.DMA((2,)),
                pltpu.SemaphoreType.DMA((count, 4)),
            ],
        ),
        input_output_aliases=aliases,
        compiler_params=pltpu.CompilerParams(vmem_limit_bytes=60 * 1024 * 1024),
        cost_estimate=pl.CostEstimate(
            flops=2 * flops, bytes_accessed=40 * 1024 * 1024, transcendentals=0
        ),
    )(expert_ids, *operands)


def on_device(
    shards,
    reps,
    layer_input,
    attention_gain,
    query_weight,
    key_weight,
    value_weight,
    output_weight,
    expert_gain,
    router_weight,
    gate_weight,
    up_weight,
    down_weight,
    lengths,
    routes,
    cotangent,
):
    me, rep = lax.axis_index("shard"), lax.axis_index("rep")
    tokens = layer_input.shape[0]
    local_experts, half = down_weight.shape[0], down_weight.shape[1]
    length = lengths[0]
    bf16, f32 = jnp.bfloat16, jnp.float32
    heads_width = (HEADS + 2 * KV) * HD
    layers = 4 if (shards == 16 and reps == 2 and local_experts == 2) else 1
    layered = layers > 1
    ring = Ring(shards, reps, layers)
    barrier = lax.optimization_barrier

    packed = jnp.concatenate([query_weight, key_weight, value_weight], axis=1)
    packed_full = lax.all_gather(packed, "shard", axis=0, tiled=True)
    packed_full, output_weight = barrier((packed_full, output_weight))
    output_full = lax.all_gather(output_weight, "shard", axis=0, tiled=True)

    def layer_swap(array, bit):
        stride = bit * (shards // layers)
        return lax.ppermute(array, "shard", [(s, s ^ stride) for s in range(shards)])

    if layered:
        own = [
            lax.dynamic_index_in_dim(weight, rep, axis=0, keepdims=False)
            for weight in (gate_weight, up_weight, down_weight)
        ]

        def owned(bits):
            return 2 * (me ^ (bits * (shards // layers))) + rep

        half_ids = [
            jnp.stack([owned(0), owned(1)]).astype(jnp.int32),
            jnp.stack([owned(2), owned(3)]).astype(jnp.int32),
        ]
    else:
        half_ids = [(me * local_experts + jnp.arange(local_experts)).astype(jnp.int32)]

    expert_ids = jnp.arange(EXPERTS, dtype=jnp.int32)
    routes_turned = routes.T
    picks = functools.reduce(
        jnp.logical_or, [routes_turned[k][None, :] == expert_ids[:, None] for k in range(TOP)]
    )
    valid = (jnp.arange(tokens, dtype=jnp.int32) < length)[:, None]
    slope_low = jnp.where(valid, cotangent, jnp.zeros_like(cotangent))
    slope = slope_low.astype(f32)
    slope_near = [jnp.concatenate([slope_low, picks.astype(bf16)], axis=0)]

    def slope_hop(*tie):
        if len(slope_near) == ring.steps:
            return tie
        arrived = ring.hop(slope_near[-1])
        arrived, *tie = barrier((arrived, *tie))
        slope_near.append(arrived)
        return tie

    inputs_f = layer_input.astype(f32)
    first_scale = lax.rsqrt(jnp.mean(inputs_f * inputs_f, axis=-1, keepdims=True) + epsilon)
    base_one = inputs_f * first_scale
    normed_one = (base_one * attention_gain).astype(bf16)
    cosine, sine = rope_tables(tokens)
    (normed_one,) = slope_hop(normed_one)
    normed_one, packed_full = slope_hop(normed_one, packed_full)
    if layered:
        packed_full, own = barrier((packed_full, own))
        next_one = [layer_swap(own[0], 1)]
        across_two = [layer_swap(own[0], 2)]
    heads = []
    for part in range(2):
        result = attention_forward(lengths, normed_one, packed_full, cosine, sine, part)
        if part == 0:
            result, packed_full = slope_hop(result, packed_full)
            if layered:
                result, packed_full, own, next_one[0] = barrier(
                    (result, packed_full, own, next_one[0])
                )
                next_one.append(layer_swap(own[1], 1))
        elif layered:
            result, own, next_one[1], across_two[0] = barrier(
                (result, own, next_one[1], across_two[0])
            )
            next_one.append(layer_swap(own[2], 1))
            across_two.append(layer_swap(own[1], 2))
        heads.append(result)
    attended = jnp.concatenate([heads[part][3] for part in range(2)], axis=1)
    residual = inputs_f + dot(attended, output_full)
    second_scale = lax.rsqrt(jnp.mean(residual * residual, axis=-1, keepdims=True) + epsilon)
    base_two = residual * second_scale
    normed_two = (base_two * expert_gain).astype(bf16)

    across_three = []
    if layered:
        normed_two, next_one[2], across_two[0], own = barrier(
            (normed_two, next_one[2], across_two[0], own)
        )
        across_two.append(layer_swap(own[2], 2))
        across_three.append(layer_swap(across_two[0], 1))

    near = [normed_two]
    while len(near) < ring.steps:
        near.append(ring.hop(near[-1]))
        if len(slope_near) < ring.steps:
            near[-1], *_ = slope_hop(near[-1])
    far = [ring.cross(block) for block in near]
    slope_far = [ring.cross(block) for block in slope_near]

    masks = jnp.stack(
        [block[tokens:] for step in range(ring.steps) for block in (slope_near[step], slope_far[step])]
    )
    earlier = jnp.triu(jnp.ones((tokens, tokens), bf16), k=1)
    all_ids = jnp.concatenate(half_ids)
    mine = jnp.take(masks.astype(f32), all_ids, axis=1, mode="clip")
    ranks = dot(mine.reshape(-1, tokens).astype(bf16), earlier).astype(jnp.int32).reshape(mine.shape)
    slots = jnp.where(mine > 0.5, ranks, ABSENT)
    count = half_ids[0].shape[0]
    half_slots = [slots[:, h * count : (h + 1) * count] for h in range(len(half_ids))]

    if layered:
        order = [(0, step) for step in range(1, ring.steps)]
        order += [(1, step % ring.steps) for step in range(1, ring.steps + 1)] + [(0, 0)]
    else:
        half_weights = [
            [w[e] for e in range(local_experts) for w in (gate_weight, up_weight, down_weight)]
        ]
        order = [(0, step) for step in range(ring.steps)]

    def expert_grads(kept):
        rows, routed, hidden, slopes = kept
        turned = (((0,), (0,)), ((), ()))
        return [
            (
                lax.dot_general(rows[e], slopes[e], turned, preferred_element_type=f32).astype(bf16),
                lax.dot_general(hidden[e], routed[e], turned, preferred_element_type=f32).astype(bf16),
            )
            for e in range(count)
        ]

    def thirds(pair):
        middle = pair[0].shape[0] // 2
        return [pair[0][:middle], pair[0][middle:], pair[1]]

    def to_owner(which):
        both = far_grads[0][which].astype(f32) + three_sum[which].astype(f32)
        return layer_swap(both.astype(bf16), 2)

    def across(array):
        return lax.ppermute(array, "rep", [(0, 1), (1, 0)])

    def finish(which):
        parts = (near_grads[0][which], two_sum[which], next_sum[which])
        sums.append(sum(g.astype(f32) for g in parts).astype(bf16))
        others.append(across(sums[-1]))

    three_sum, next_sum, two_sum, sums, others = [], [], [], [], []
    kept = [None] * len(half_ids)
    back_parts = [([], []) for _ in range(ring.steps)]
    mix_parts = [([], []) for _ in range(ring.steps)]
    total, next_step, last = None, 1, None
    for turn, (which, step) in enumerate(order):
        tokens_now = near[step]
        if last is not None:
            tokens_now, last = barrier((tokens_now, last))
        if layered:
            now = [*own, *next_one] if which == 0 else [*across_two, *across_three]
        else:
            now = half_weights[0]
        results = experts_pair(
            step,
            ring.steps,
            half_ids[which],
            tokens_now,
            far[step],
            slope_near[step],
            slope_far[step],
            half_slots[which],
            (router_weight, *now),
            kept[which],
        )
        kept[which] = results[4:8]
        for side in range(2):
            back_parts[step][side].append(results[side])
            mix_parts[step][side].append(results[2 + side])
        last = results[2]
        if layered and turn == 0:
            last, across_two[1], across_three[0] = barrier((last, across_two[1], across_three[0]))
            across_three.append(layer_swap(across_two[1], 1))
        elif layered and turn == 1:
            last, across_two[2], across_three[1] = barrier((last, across_two[2], across_three[1]))
            across_three.append(layer_swap(across_two[2], 1))
        if layered and (which, step) == (1, 0):
            far_grads = [thirds(pair) for pair in expert_grads(kept[1])]
            last, far_grads = barrier((last, far_grads))
            three_sum.append(layer_swap(far_grads[1][0], 1))
        elif layered and (which, step) == (0, 0):
            last, kept[0], three_sum[0] = barrier((last, kept[0], three_sum[0]))
            two_sum.append(to_owner(0))
            three_sum += [layer_swap(far_grads[1][at], 1) for at in (1, 2)]
        mix_parts[step][0][-1] = last
        while next_step < ring.steps and len(back_parts[next_step][0]) == len(half_ids):
            more = () if total is None else (total,)
            total = ring.hop(ring.part_sum(*back_parts[next_step], *more).astype(bf16))
            next_step += 1

    if layered:
        near_grads = [thirds(pair) for pair in expert_grads(kept[0])]
        total, near_grads, three_sum[1], three_sum[2] = barrier(
            (total, near_grads, three_sum[1], three_sum[2])
        )
        two_sum += [to_owner(1), to_owner(2)]
        next_sum += [layer_swap(near_grads[1][which], 1) for which in range(3)]
        back = ring.part_sum(*back_parts[0], total)
    else:
        back = ring.part_sum(*back_parts[0], total)
        whole_grads = expert_grads(kept[0])
        back, whole_grads = barrier((back, whole_grads))
    normed_slope = back[:tokens]
    gate_slope = back[tokens : tokens + EXPERTS] + back[tokens + EXPERTS :]

    logits = lax.dot_general(
        router_weight, normed_two, (((0,), (1,)), ((), ())), preferred_element_type=f32
    )
    kept_logits = jnp.where(picks, logits, masked_score)
    powered = jnp.where(
        picks, jnp.exp(kept_logits - jnp.max(kept_logits, axis=0, keepdims=True)), 0.0
    )
    gates = powered / jnp.sum(powered, axis=0, keepdims=True)
    mean_slope = jnp.sum(gates * gate_slope, axis=0, keepdims=True)
    logit_slope = (gates * (gate_slope - mean_slope)).astype(bf16)
    router_grad = dot(logit_slope, normed_two)
    normed_slope = normed_slope + lax.dot_general(
        logit_slope, router_weight, (((0,), (1,)), ((), ())), preferred_element_type=f32
    )

    def mix_hop(step, total):
        more = () if total is None else (total,)
        return ring.hop(ring.part_sum(*mix_parts[step], *more).astype(bf16))

    expert_gain_grad = jnp.sum(normed_slope * base_two, axis=0)
    scaled_two = normed_slope * expert_gain
    residual_slope = (
        slope
        + second_scale * scaled_two
        - base_two
        * second_scale
        * second_scale
        * jnp.mean(scaled_two * residual, axis=-1, keepdims=True)
    )
    branch_slope = residual_slope.astype(bf16)
    output_grad = lax.dot_general(
        attended, branch_slope, (((0,), (0,)), ((), ())), preferred_element_type=f32
    ).astype(bf16)
    attended_slope = jnp.einsum(
        "sd,cd->sc", branch_slope, output_full, preferred_element_type=f32
    ).astype(bf16)
    output_owned = lax.psum_scatter(output_grad, "shard", scatter_dimension=0, tiled=True)

    attended_slope, mix_parts = barrier((attended_slope, mix_parts))
    mix = mix_hop(1, None)
    slopes_out = []
    mix_step = 2
    for part in range(2):
        if part > 0:
            attended_slope, mix = barrier((attended_slope, mix))
            if mix_step < ring.steps:
                mix = mix_hop(mix_step, mix)
                mix_step += 1
        if layered:
            attended_slope, next_sum[part] = barrier((attended_slope, next_sum[part]))
            if part == 1:
                attended_slope, two_sum[0] = barrier((attended_slope, two_sum[0]))
                finish(0)
        queries, keys, values, _, log_totals = heads[part]
        slopes_out.append(
            attention_backward(
                lengths, queries, keys, values, attended_slope, log_totals, cosine, sine, part
            )
        )
        if part == 0:
            attended_slope, slopes_out[0] = barrier((attended_slope, slopes_out[0]))
    pre_slopes = jnp.concatenate(
        [slopes_out[part][which] for which in range(3) for part in range(2)], axis=1
    )
    pre_slopes, mix = barrier((pre_slopes, mix))
    if layered:
        pre_slopes, next_sum[2] = barrier((pre_slopes, next_sum[2]))
    while mix_step < ring.steps:
        mix = mix_hop(mix_step, mix)
        mix_step += 1
    input_grad = lax.dot_general(
        normed_one, pre_slopes, (((0,), (0,)), ((), ())), preferred_element_type=f32
    ).astype(bf16)
    input_owned = lax.psum_scatter(input_grad, "shard", scatter_dimension=0, tiled=True)
    normed_one_slope = jnp.einsum(
        "sc,dc->sd", pre_slopes, packed_full, preferred_element_type=f32
    )
    attention_gain_grad = jnp.sum(normed_one_slope * base_one, axis=0)
    gain_sum = jnp.concatenate(
        [attention_gain_grad[None], expert_gain_grad[None], router_grad], axis=0
    )
    for axis, size in (("rep", reps), ("shard", shards)):
        far_bit = 1
        while far_bit < size:
            gain_sum = gain_sum + lax.ppermute(
                gain_sum, axis, [(place, place ^ far_bit) for place in range(size)]
            )
            far_bit *= 2
    scaled_one = normed_one_slope * attention_gain
    input_slope = (
        residual_slope
        + first_scale * scaled_one
        - base_one
        * first_scale
        * first_scale
        * jnp.mean(scaled_one * inputs_f, axis=-1, keepdims=True)
    )
    input_gradient = input_slope.astype(bf16)
    if layered:
        input_gradient, two_sum[1] = barrier((input_gradient, two_sum[1]))
        finish(1)
        gain_sum, two_sum[2] = barrier((gain_sum, two_sum[2]))
        finish(2)
    layer_output = (residual + ring.part_sum(*mix_parts[0], mix)).astype(bf16)

    def rep_sum(*arrays):
        if reps != 2:
            return lax.psum(tuple(array.astype(f32) for array in arrays), "rep")
        low = [array.astype(bf16) for array in arrays]
        return tuple(a.astype(f32) + across(a).astype(f32) for a in low)

    if layered:
        whole = [
            jnp.stack([jnp.where(rep == 0, a, b), jnp.where(rep == 0, b, a)])
            for a, b in zip([x.astype(f32) for x in sums], [x.astype(f32) for x in others])
        ]
        in_sum, down_sum = jnp.concatenate(whole[:2], axis=1), whole[2]
    else:
        in_sum, down_sum = rep_sum(
            jnp.stack([g[0] for g in whole_grads]), jnp.stack([g[1] for g in whole_grads])
        )
    gain_sum, output_owned, input_owned = barrier((gain_sum, output_owned, input_owned))
    output_sum, input_sum = rep_sum(output_owned, input_owned)
    return (
        layer_output,
        input_gradient,
        gain_sum[0],
        input_sum[:, : HEADS * HD],
        input_sum[:, HEADS * HD : (HEADS + KV) * HD],
        input_sum[:, (HEADS + KV) * HD :],
        output_sum,
        gain_sum[1],
        gain_sum[2:].T,
        in_sum[..., :half],
        in_sum[..., half:],
        down_sum,
    )


def solution(mesh):
    return jax.shard_map(
        functools.partial(on_device, mesh.shape["shard"], mesh.shape["rep"]),
        mesh=mesh,
        in_specs=(
            P(("shard", "rep"), None),
            P(),
            P("shard", None),
            P("shard", None),
            P("shard", None),
            P("shard", None),
            P(),
            P(),
            P("shard", None, None),
            P("shard", None, None),
            P("shard", None, None),
            P(("shard", "rep")),
            P(("shard", "rep"), None),
            P(("shard", "rep"), None),
        ),
        out_specs=(
            P(("shard", "rep"), None),
            P(("shard", "rep"), None),
            P(),
            P("shard", None),
            P("shard", None),
            P("shard", None),
            P("shard", None),
            P(),
            P(),
            P("shard", None, None),
            P("shard", None, None),
            P("shard", None, None),
        ),
        check_vma=False,
    )
```

```python
import functools

import jax
import jax.numpy as jnp
import numpy as np
from jax import lax
from jax.experimental import pallas as pl
from jax.experimental.pallas import tpu as pltpu
from jax.sharding import PartitionSpec as P

D = 1024
HEADS = 16
KV = 8
HD = 64
EXPERTS = 32
TOP = 8
CAP = 288
ABSENT = -100000


epsilon = 1e-06
masked_score = -1e30
rotary_base = 10000.0


def chip_cycle(count):
    if count % 4 == 0 and count >= 8:
        wide = count // 4
        tall = 4
    else:
        return list(range(count))
    if wide == 1:
        return list(range(count))
    order = [row * wide for row in range(tall)]
    for step, row in enumerate(reversed(range(tall))):
        columns = range(1, wide) if step % 2 == 0 else reversed(range(1, wide))
        order += [row * wide + column for column in columns]
    return order


class Ring:
    def __init__(self, shards, reps, layers):
        if layers > 1:
            wide = shards // (2 * layers)
            cells = [
                [(layer * wide + x, y) for y in range(reps) for x in (range(wide) if y % 2 == 0 else reversed(range(wide)))]
                for layer in range(layers)
            ]
        else:
            cells = [[(chip, rep) for chip in chip_cycle(shards // 2)] for rep in range(reps)]
        self.steps = len(cells[0])
        self.forward, self.swap = [], []

        def device(chip, core):
            return (2 * chip[0] + core) * reps + chip[1]

        for cell in cells:
            for place, here in enumerate(cell):
                there = cell[(place + 1) % len(cell)]
                self.forward += [
                    (device(here, 0), device(there, 0)),
                    (device(there, 1), device(here, 1)),
                ]
                self.swap += [(device(here, 0), device(here, 1)), (device(here, 1), device(here, 0))]

    def hop(self, array):
        return lax.ppermute(array, ("shard", "rep"), self.forward)

    def cross(self, array):
        return lax.ppermute(array, ("shard", "rep"), self.swap)

    def part_sum(self, near, far, *more):
        far = far[0] if len(far) == 1 else sum(part.astype(jnp.float32) for part in far)
        parts = [*near, self.cross(far.astype(jnp.bfloat16)), *more]
        return sum(part.astype(jnp.float32) for part in parts)


def rope_tables(tokens):
    halfway = HD // 2
    index_float = jnp.arange(halfway, dtype=jnp.float32)
    frequency = jnp.exp(-jnp.log(rotary_base) * index_float * 2.0 / HD)
    angle = jnp.arange(tokens, dtype=jnp.float32)[:, None] * frequency[None, :]
    cosine, sine = jnp.cos(angle), jnp.sin(angle)
    return (
        jnp.concatenate([cosine] * 4, axis=1),
        jnp.concatenate([-sine, sine, -sine, sine], axis=1),
    )


def dot(l,r): return jnp.dot(l,r,preferred_element_type=jnp.float32)
def dot_nt(l,r): return lax.dot_general(l,r,(((1,),(1,)),((),())),preferred_element_type=jnp.float32)
def dot_tn(l,r): return lax.dot_general(l,r,(((0,),(0,)),((),())),preferred_element_type=jnp.float32)

def swap_halves(values):
    parts=[]
    for start in range(0, values.shape[1], 128):
        part=values[:,start:start+128]
        lane=lax.broadcasted_iota(jnp.int32,part.shape,1)
        parts.append(jnp.where(lane % HD < HD//2, pltpu.roll(part,128-HD//2,1), pltpu.roll(part,HD//2,1)))
    return parts[0] if len(parts)==1 else jnp.concatenate(parts,axis=1)

def tile(table,width):
    return table if width==128 else jnp.concatenate([table]*(width//128),axis=1)

def forward_kernel(block, length_ref, normed_ref, wq_ref, wk_ref, wv_ref, cos_ref, sin_ref,
                   q_ref,k_ref,v_ref,out_ref,total_ref):
    tokens=normed_ref.shape[0]
    length=length_ref[0]
    cos,sin=cos_ref[...],sin_ref[...]
    bf16=jnp.bfloat16
    x=normed_ref[...]
    q=dot(x,wq_ref[...])
    q=q*tile(cos,q.shape[1])+swap_halves(q)*tile(sin,q.shape[1])
    q_ref[...]=(q.astype(bf16).astype(jnp.float32)*(HD**-0.5)).astype(bf16)
    k=dot(x,wk_ref[...])
    k_ref[...]=(k*cos+swap_halves(k)*sin).astype(bf16)
    v_ref[...]=dot(x,wv_ref[...]).astype(bf16)
    groups=HEADS//KV
    for head in range(2):
        for i in range(tokens//block):
            rows=slice(i*block,(i+1)*block)
            span=(i+1)*block
            keys=k_ref[:span,head*HD:(head+1)*HD]
            vals=v_ref[:span,head*HD:(head+1)*HD]
            qs=jnp.concatenate([q_ref[rows,(head*groups+h)*HD:(head*groups+h+1)*HD] for h in range(groups)],axis=0)
            s=dot_nt(keys,qs)
            key_place=lax.broadcasted_iota(jnp.int32,s.shape,0)
            query_place=lax.broadcasted_iota(jnp.int32,s.shape,1) % block + i*block
            s=jnp.where(key_place<=jnp.minimum(query_place,length-1),s,masked_score)
            top=jnp.max(s,axis=0,keepdims=True)
            p=jnp.exp(s-top)
            total=jnp.sum(p,axis=0,keepdims=True)
            p=(p*(1.0/total)).astype(bf16)
            o=dot_tn(p,vals)
            log_total=top+jnp.log(total)
            for h in range(groups):
                at=head*groups+h
                out_ref[rows,at*HD:(at+1)*HD]=o[h*block:(h+1)*block].astype(bf16)
                total_ref[0,at:at+1,rows]=log_total[:,h*block:(h+1)*block]

def attention_forward(length, normed, packed, cos, sin, part, block=256):
    tokens,width=normed.shape
    qw=HEADS*HD//4; kw=KV*HD//4
    bf16=jnp.bfloat16
    qb=HEADS*HD//kw; vb=(HEADS+KV)*HD//kw
    return pl.pallas_call(
        functools.partial(forward_kernel,block),
        out_shape=[jax.ShapeDtypeStruct((tokens,2*qw),bf16),jax.ShapeDtypeStruct((tokens,2*kw),bf16),jax.ShapeDtypeStruct((tokens,2*kw),bf16),
                   jax.ShapeDtypeStruct((tokens,2*qw),bf16),jax.ShapeDtypeStruct((2,HEADS//4,tokens),jnp.float32)],
        grid_spec=pltpu.PrefetchScalarGridSpec(num_scalar_prefetch=1,grid=(2,),
            in_specs=[pl.BlockSpec((tokens,width),lambda g,l:(0,0)),
                      pl.BlockSpec((width,qw),lambda g,l:(0,g+2*part)),
                      pl.BlockSpec((width,kw),lambda g,l:(0,qb+g+2*part)),
                      pl.BlockSpec((width,kw),lambda g,l:(0,vb+g+2*part)),
                      pl.BlockSpec((tokens,128),lambda g,l:(0,0)),pl.BlockSpec((tokens,128),lambda g,l:(0,0))],
            out_specs=[pl.BlockSpec((tokens,qw),lambda g,l:(0,g)),pl.BlockSpec((tokens,kw),lambda g,l:(0,g)),pl.BlockSpec((tokens,kw),lambda g,l:(0,g)),
                       pl.BlockSpec((tokens,qw),lambda g,l:(0,g)),pl.BlockSpec((1,HEADS//4,tokens),lambda g,l:(g,0,0))]),
        compiler_params=pltpu.CompilerParams(vmem_limit_bytes=40*1024*1024),
        cost_estimate=pl.CostEstimate(flops=30*10**9,bytes_accessed=20*1024*1024,transcendentals=0),
    )(length,normed,packed,packed,packed,cos,sin)

def backward_kernel(block,length_ref,q_ref,k_ref,v_ref,slope_ref,total_ref,cos_ref,sin_ref,dq_ref,dk_ref,dv_ref,dq_s,dk_s,dv_s):
    tokens=q_ref.shape[0]
    length=length_ref[0]
    bf16=jnp.bfloat16
    groups=HEADS//KV
    for head in range(2):
        lanes=slice(head*HD,(head+1)*HD)
        for i in reversed(range(tokens//block)):
            rows=slice(i*block,(i+1)*block)
            span=(i+1)*block
            keys=k_ref[:span,lanes]; vals=v_ref[:span,lanes]
            heads=[slice((head*groups+h)*HD,(head*groups+h+1)*HD) for h in range(groups)]
            qs=jnp.concatenate([q_ref[rows,at] for at in heads],axis=0)
            slopes=jnp.concatenate([slope_ref[rows,at] for at in heads],axis=0)
            log_total=jnp.concatenate([total_ref[0,head*groups+h:head*groups+h+1,rows] for h in range(groups)],axis=1)
            s=dot_nt(keys,qs)
            key_place=lax.broadcasted_iota(jnp.int32,s.shape,0)
            query_place=lax.broadcasted_iota(jnp.int32,s.shape,1) % block + i*block
            s=jnp.where(key_place<=jnp.minimum(query_place,length-1),s,masked_score)
            w=jnp.exp(s-log_total)
            ps=dot_nt(vals,slopes)
            centre=jnp.sum(w*ps,axis=0,keepdims=True)
            ds=(w*(ps-centre)).astype(bf16)
            dq=dot_tn(ds,keys)
            dk=dot(ds,qs)
            dv=dot(w.astype(bf16),slopes)
            for h in range(groups):
                dq_s[rows,heads[h]]=dq[h*block:(h+1)*block]*(HD**-0.5)
            if i==tokens//block-1:
                dk_s[:,lanes]=dk; dv_s[:,lanes]=dv
            else:
                dk_s[:span,lanes]+=dk; dv_s[:span,lanes]+=dv
    cos,sin=cos_ref[...],sin_ref[...]
    dq=dq_s[...]
    dq_ref[...]=(dq*tile(cos,dq.shape[1])-swap_halves(dq)*tile(sin,dq.shape[1])).astype(bf16)
    dk=dk_s[...]
    dk_ref[...]=(dk*cos-swap_halves(dk)*sin).astype(bf16)
    dv_ref[...]=dv_s[...].astype(bf16)

def attention_backward(length,q,k,v,slope,total,cos,sin,part,block=256):
    tokens=q.shape[0]
    qw=HEADS*HD//4; kw=KV*HD//4
    bf16=jnp.bfloat16
    qs=pl.BlockSpec((tokens,qw),lambda g,l:(0,g)); ks=pl.BlockSpec((tokens,kw),lambda g,l:(0,g)); cs=pl.BlockSpec((tokens,128),lambda g,l:(0,0))
    return pl.pallas_call(
        functools.partial(backward_kernel,block),
        out_shape=[jax.ShapeDtypeStruct((tokens,2*qw),bf16),jax.ShapeDtypeStruct((tokens,2*kw),bf16),jax.ShapeDtypeStruct((tokens,2*kw),bf16)],
        grid_spec=pltpu.PrefetchScalarGridSpec(num_scalar_prefetch=1,grid=(2,),
            in_specs=[qs,ks,ks,pl.BlockSpec((tokens,qw),lambda g,l:(0,g+2*part)),pl.BlockSpec((1,HEADS//4,tokens),lambda g,l:(g,0,0)),cs,cs],
            out_specs=[qs,ks,ks],
            scratch_shapes=[pltpu.VMEM((tokens,qw),jnp.float32),pltpu.VMEM((tokens,kw),jnp.float32),pltpu.VMEM((tokens,kw),jnp.float32)]),
        compiler_params=pltpu.CompilerParams(vmem_limit_bytes=40*1024*1024),
        cost_estimate=pl.CostEstimate(flops=20*10**9,bytes_accessed=10*1024*1024,transcendentals=0),
    )(length,q,k,v,slope,total,cos,sin)

def pair_kernel(
    count,
    step,
    chained,
    ids_ref,
    tokens_a,
    tokens_b,
    slope_a,
    slope_b,
    row_a,
    row_b,
    mask_a,
    mask_b,
    router_ref,
    *rest,
):
    weights, rest = rest[: 3 * count], rest[3 * count :]
    rest = rest[4:] if chained else rest
    back_out, mix_out, kept_out, rest = rest[0:2], rest[2:4], rest[4:8], rest[8:]
    blocks, backs, mixes, gates_in, ups_in, downs_in, rest = *rest[:6], rest[6:]
    rows_buf, routed_buf, hidden_buf, slopes_buf, raw_buf, mixed_rows, back_rows, rest = (
        *rest[:7],
        rest[7:],
    )
    load_sems, weight_sems, back_sems, mix_sems, kept_sems = rest
    tokens = blocks.shape[1]
    pair_rows = 2 * CAP
    bf16, f32 = jnp.bfloat16, jnp.float32
    sources = (tokens_a, slope_a, tokens_b, slope_b)

    def load(which):
        return pltpu.make_async_copy(
            sources[which].at[pl.ds(0, tokens)], blocks.at[which], load_sems.at[which]
        )

    def load_weight(e, which):
        target = (gates_in, ups_in, downs_in)[which].at[e]
        return pltpu.make_async_copy(weights[3 * e + which], target, weight_sems.at[e, which])

    stores = []

    def store(source, target, sem):
        stores.append(pltpu.make_async_copy(source, target, sem))
        stores[-1].start()

    def keep(e, which):
        source = (rows_buf, routed_buf, hidden_buf, slopes_buf)[which].at[e]
        target = kept_out[which].at[e, pl.ds(step * pair_rows, pair_rows)]
        store(source, target, kept_sems.at[e, which])

    for which in (0, 2, 1, 3):
        load(which).start()
    for e in range(count):
        for which in range(3):
            load_weight(e, which).start()

    taken, picks, chosen = [], [], []
    for side, (row_ref, mask_ref) in enumerate(((row_a, mask_a), (row_b, mask_b))):
        place = lax.broadcasted_iota(jnp.int32, (CAP, tokens), 0)
        taken.append([row_ref[0, e : e + 1] == place for e in range(count)])
        hits = [jnp.where(hit, 1.0, 0.0).astype(bf16) for hit in taken[side]]
        picks.append(hits[0] if count == 1 else jnp.concatenate(hits, axis=0))
        chosen.append(dot_nt(picks[side], mask_ref[...]))
        load(2 * side).wait()
        rows = dot(picks[side], blocks[2 * side]).astype(bf16)
        for e in range(count):
            rows_buf[e, side * CAP : (side + 1) * CAP] = rows[e * CAP : (e + 1) * CAP]
    for e in range(count):
        keep(e, 0)
    for side in range(2):
        load(2 * side + 1).wait()
        rows = dot(picks[side], blocks[2 * side + 1]).astype(bf16)
        for e in range(count):
            raw_buf[e, side * CAP : (side + 1) * CAP] = rows[e * CAP : (e + 1) * CAP]
    homeward = [[], []]
    for e in range(count):
        rows = rows_buf[e]
        marks = jnp.concatenate([chosen[side][e * CAP : (e + 1) * CAP] for side in range(2)], axis=0)
        logits = dot(rows, router_ref[...])
        kept = jnp.where(marks > 0.5, logits, masked_score)
        top = jnp.max(kept, axis=-1, keepdims=True)
        powered = jnp.exp(kept - top) * marks
        total = jnp.sum(powered, axis=-1, keepdims=True)
        lane = lax.broadcasted_iota(jnp.int32, powered.shape, 1)
        mine = lane == ids_ref[e]
        gate = jnp.sum(jnp.where(mine, powered, 0.0), axis=-1, keepdims=True) / jnp.where(
            total > 0.0, total, 1.0
        )
        slope_rows = raw_buf[e].astype(f32)
        routed = (gate * slope_rows).astype(bf16)
        routed_buf[e] = routed
        keep(e, 1)
        for which in range(3):
            load_weight(e, which).wait()
        gate_part = dot(rows, gates_in[e])
        up_part = dot(rows, ups_in[e])
        hidden_slope = dot_nt(routed, downs_in[e])
        sigma = 1.0 / (1.0 + jnp.exp(-gate_part))
        silu = gate_part * sigma
        hidden = (silu * up_part).astype(bf16)
        hidden_buf[e] = hidden
        keep(e, 2)
        gate_back = (hidden_slope * up_part * sigma * (1.0 + gate_part * (1.0 - sigma))).astype(bf16)
        up_back = (hidden_slope * silu).astype(bf16)
        half = gate_back.shape[1]
        slopes_buf[e, :, :half] = gate_back
        slopes_buf[e, :, half:] = up_back
        keep(e, 3)
        out = dot(hidden, downs_in[e]).astype(bf16).astype(f32)
        back = (dot_nt(gate_back, gates_in[e]) + dot_nt(up_back, ups_in[e])).astype(bf16)
        gate_slope = jnp.sum(out * slope_rows, axis=-1, keepdims=True)
        mixed = (gate * out).astype(bf16)
        for side in range(2):
            part = slice(side * CAP, (side + 1) * CAP)
            homeward[side].append(
                jnp.sum(jnp.where(taken[side][e], gate_slope[part], 0.0), axis=0, keepdims=True)
            )
            mixed_rows[side, e * CAP : (e + 1) * CAP] = mixed[part]
            back_rows[side, e * CAP : (e + 1) * CAP] = back[part]
    for side, row_ref in enumerate((row_a, row_b)):
        backs[side, :tokens] = dot_tn(picks[side], back_rows[side]).astype(bf16)
        row = lax.broadcasted_iota(jnp.int32, (EXPERTS, tokens), 0)
        whole = jnp.zeros(row.shape, f32)
        for e in range(count):
            whole = jnp.where(row == ids_ref[e], homeward[side][e], whole)
        high = whole.astype(bf16)
        backs[side, tokens : tokens + EXPERTS] = high
        backs[side, tokens + EXPERTS :] = (whole - high.astype(f32)).astype(bf16)
        store(backs.at[side], back_out[side], back_sems.at[side])
        mixes[side] = dot_tn(picks[side], mixed_rows[side]).astype(bf16)
        store(mixes.at[side], mix_out[side], mix_sems.at[side])
    for copy in stores:
        copy.wait()


def experts_pair(step, steps, expert_ids, ta, tb, sa, sb, slots, weights, kept):
    router, *weights = weights
    tokens, width = ta.shape
    count, half = len(weights) // 3, weights[2].shape[0]
    bf16 = jnp.bfloat16
    chained = kept is not None
    once = pl.Buffered(1)
    back_rows = tokens + 2 * EXPERTS

    def block(rows, at=0):
        return pl.BlockSpec((rows, width), lambda e, w: (at, 0), pipeline_mode=once)

    anywhere = pl.BlockSpec(memory_space=pl.ANY)
    in_specs = [anywhere] * 4
    in_specs += [
        pl.BlockSpec((1, count, tokens), lambda e, w, i=i: (2 * step + i, 0, 0), pipeline_mode=once)
        for i in range(2)
    ]
    in_specs += [block(EXPERTS, tokens // EXPERTS)] * 2
    in_specs += [pl.BlockSpec((width, EXPERTS), lambda e, w: (0, 0), pipeline_mode=once)]
    in_specs += [anywhere] * len(weights)
    rows = 2 * CAP
    columns = (width, width, half, 2 * half)
    shapes = [jax.ShapeDtypeStruct((back_rows, width), bf16)] * 2
    shapes += [jax.ShapeDtypeStruct((tokens, width), bf16)] * 2
    shapes += [jax.ShapeDtypeStruct((count, steps * rows, column), bf16) for column in columns]
    out_specs = [anywhere] * 8
    operands = [ta, tb, sa, sb, slots, slots, sa, sb, router, *weights]
    aliases = {}
    if chained:
        first = 1 + len(operands)
        operands += list(kept)
        in_specs += [anywhere] * 4
        aliases = {first + p: 4 + p for p in range(4)}
    flops = count * 2 * rows * (4 * tokens * width + 6 * width * half)
    return pl.pallas_call(
        functools.partial(pair_kernel, count, step, chained),
        out_shape=shapes,
        grid_spec=pltpu.PrefetchScalarGridSpec(
            num_scalar_prefetch=1,
            grid=(1,),
            in_specs=in_specs,
            out_specs=out_specs,
            scratch_shapes=[
                pltpu.VMEM((4, tokens, width), bf16),
                pltpu.VMEM((2, back_rows, width), bf16),
                pltpu.VMEM((2, tokens, width), bf16),
                pltpu.VMEM((count, width, half), bf16),
                pltpu.VMEM((count, width, half), bf16),
                pltpu.VMEM((count, half, width), bf16),
                *[pltpu.VMEM((count, rows, column), bf16) for column in columns],
                pltpu.VMEM((count, rows, width), bf16),
                pltpu.VMEM((2, count * CAP, width), bf16),
                pltpu.VMEM((2, count * CAP, width), bf16),
                pltpu.SemaphoreType.DMA((4,)),
                pltpu.SemaphoreType.DMA((count, 3)),
                pltpu.SemaphoreType.DMA((2,)),
                pltpu.SemaphoreType.DMA((2,)),
                pltpu.SemaphoreType.DMA((count, 4)),
            ],
        ),
        input_output_aliases=aliases,
        compiler_params=pltpu.CompilerParams(vmem_limit_bytes=60 * 1024 * 1024),
        cost_estimate=pl.CostEstimate(
            flops=2 * flops, bytes_accessed=40 * 1024 * 1024, transcendentals=0
        ),
    )(expert_ids, *operands)


def on_device(
    shards,
    reps,
    layer_input,
    attention_gain,
    query_weight,
    key_weight,
    value_weight,
    output_weight,
    expert_gain,
    router_weight,
    gate_weight,
    up_weight,
    down_weight,
    lengths,
    routes,
    cotangent,
):
    me, rep = lax.axis_index("shard"), lax.axis_index("rep")
    tokens = layer_input.shape[0]
    local_experts, half = down_weight.shape[0], down_weight.shape[1]
    length = lengths[0]
    bf16, f32 = jnp.bfloat16, jnp.float32
    heads_width = (HEADS + 2 * KV) * HD
    layers = 4 if (shards == 16 and reps == 2 and local_experts == 2) else 1
    layered = layers > 1
    ring = Ring(shards, reps, layers)
    barrier = lax.optimization_barrier

    packed = jnp.concatenate([query_weight, key_weight, value_weight], axis=1)
    packed_full = lax.all_gather(packed, "shard", axis=0, tiled=True)
    packed_full, output_weight = barrier((packed_full, output_weight))
    output_full = lax.all_gather(output_weight, "shard", axis=0, tiled=True)

    def layer_swap(array, bit):
        stride = bit * (shards // layers)
        return lax.ppermute(array, "shard", [(s, s ^ stride) for s in range(shards)])

    if layered:
        own = [
            lax.dynamic_index_in_dim(weight, rep, axis=0, keepdims=False)
            for weight in (gate_weight, up_weight, down_weight)
        ]

        def owned(bits):
            return 2 * (me ^ (bits * (shards // layers))) + rep

        half_ids = [
            jnp.stack([owned(0), owned(1)]).astype(jnp.int32),
            jnp.stack([owned(2), owned(3)]).astype(jnp.int32),
        ]
    else:
        half_ids = [(me * local_experts + jnp.arange(local_experts)).astype(jnp.int32)]

    expert_ids = jnp.arange(EXPERTS, dtype=jnp.int32)
    routes_turned = routes.T
    picks = functools.reduce(
        jnp.logical_or, [routes_turned[k][None, :] == expert_ids[:, None] for k in range(TOP)]
    )
    valid = (jnp.arange(tokens, dtype=jnp.int32) < length)[:, None]
    slope_low = jnp.where(valid, cotangent, jnp.zeros_like(cotangent))
    slope = slope_low.astype(f32)
    slope_near = [jnp.concatenate([slope_low, picks.astype(bf16)], axis=0)]

    def slope_hop(*tie):
        if len(slope_near) == ring.steps:
            return tie
        arrived = ring.hop(slope_near[-1])
        arrived, *tie = barrier((arrived, *tie))
        slope_near.append(arrived)
        return tie

    inputs_f = layer_input.astype(f32)
    first_scale = lax.rsqrt(jnp.mean(inputs_f * inputs_f, axis=-1, keepdims=True) + epsilon)
    base_one = inputs_f * first_scale
    normed_one = (base_one * attention_gain).astype(bf16)
    cosine, sine = rope_tables(tokens)
    (normed_one,) = slope_hop(normed_one)
    normed_one, packed_full = slope_hop(normed_one, packed_full)
    if layered:
        packed_full, own = barrier((packed_full, own))
        next_one = [layer_swap(own[0], 1)]
        across_two = [layer_swap(own[0], 2)]
    heads = []
    for part in range(2):
        result = attention_forward(lengths, normed_one, packed_full, cosine, sine, part)
        if part == 0:
            result, packed_full = slope_hop(result, packed_full)
            if layered:
                result, packed_full, own, next_one[0] = barrier(
                    (result, packed_full, own, next_one[0])
                )
                next_one.append(layer_swap(own[1], 1))
        elif layered:
            result, own, next_one[1], across_two[0] = barrier(
                (result, own, next_one[1], across_two[0])
            )
            next_one.append(layer_swap(own[2], 1))
            across_two.append(layer_swap(own[1], 2))
        heads.append(result)
    attended = jnp.concatenate([heads[part][3] for part in range(2)], axis=1)
    residual = inputs_f + dot(attended, output_full)
    second_scale = lax.rsqrt(jnp.mean(residual * residual, axis=-1, keepdims=True) + epsilon)
    base_two = residual * second_scale
    normed_two = (base_two * expert_gain).astype(bf16)

    across_three = []
    if layered:
        normed_two, next_one[2], across_two[0], own = barrier(
            (normed_two, next_one[2], across_two[0], own)
        )
        across_two.append(layer_swap(own[2], 2))
        across_three.append(layer_swap(across_two[0], 1))

    near = [normed_two]
    while len(near) < ring.steps:
        near.append(ring.hop(near[-1]))
        if len(slope_near) < ring.steps:
            near[-1], *_ = slope_hop(near[-1])
    far = [ring.cross(block) for block in near]
    slope_far = [ring.cross(block) for block in slope_near]

    masks = jnp.stack(
        [block[tokens:] for step in range(ring.steps) for block in (slope_near[step], slope_far[step])]
    )
    earlier = jnp.triu(jnp.ones((tokens, tokens), bf16), k=1)
    all_ids = jnp.concatenate(half_ids)
    mine = jnp.take(masks.astype(f32), all_ids, axis=1, mode="clip")
    ranks = dot(mine.reshape(-1, tokens).astype(bf16), earlier).astype(jnp.int32).reshape(mine.shape)
    slots = jnp.where(mine > 0.5, ranks, ABSENT)
    count = half_ids[0].shape[0]
    half_slots = [slots[:, h * count : (h + 1) * count] for h in range(len(half_ids))]

    if layered:
        order = [(0, step) for step in range(ring.steps - 1)]
        order += [(1, step % ring.steps) for step in range(1, ring.steps + 1)]
        order += [(0, ring.steps - 1)]
    else:
        half_weights = [
            [w[e] for e in range(local_experts) for w in (gate_weight, up_weight, down_weight)]
        ]
        order = [(0, step) for step in range(ring.steps)]

    def expert_grads(kept):
        rows, routed, hidden, slopes = kept
        turned = (((0,), (0,)), ((), ()))
        return [
            (
                lax.dot_general(rows[e], slopes[e], turned, preferred_element_type=f32).astype(bf16),
                lax.dot_general(hidden[e], routed[e], turned, preferred_element_type=f32).astype(bf16),
            )
            for e in range(count)
        ]

    def thirds(pair):
        middle = pair[0].shape[0] // 2
        return [pair[0][:middle], pair[0][middle:], pair[1]]

    def to_owner(which):
        both = far_grads[0][which].astype(f32) + three_sum[which].astype(f32)
        return layer_swap(both.astype(bf16), 2)

    def across(array):
        return lax.ppermute(array, "rep", [(0, 1), (1, 0)])

    def finish(which):
        parts = (near_grads[0][which], two_sum[which], next_sum[which])
        sums.append(sum(g.astype(f32) for g in parts).astype(bf16))
        others.append(across(sums[-1]))

    three_sum, next_sum, two_sum, sums, others = [], [], [], [], []
    kept = [None] * len(half_ids)
    back_parts = [([], []) for _ in range(ring.steps)]
    mix_parts = [([], []) for _ in range(ring.steps)]
    total, totals, next_step, last = None, [], 1, None
    for turn, (which, step) in enumerate(order):
        tokens_now = near[step]
        if last is not None:
            tokens_now, last = barrier((tokens_now, last))
        if layered:
            now = [*own, *next_one] if which == 0 else [*across_two, *across_three]
        else:
            now = half_weights[0]
        results = experts_pair(
            step,
            ring.steps,
            half_ids[which],
            tokens_now,
            far[step],
            slope_near[step],
            slope_far[step],
            half_slots[which],
            (router_weight, *now),
            kept[which],
        )
        kept[which] = results[4:8]
        for side in range(2):
            back_parts[step][side].append(results[side])
            mix_parts[step][side].append(results[2 + side])
        last = results[2]
        if layered and turn == 0:
            last, across_two[1], across_three[0] = barrier((last, across_two[1], across_three[0]))
            across_three.append(layer_swap(across_two[1], 1))
        elif layered and turn == 1:
            last, across_two[2], across_three[1] = barrier((last, across_two[2], across_three[1]))
            across_three.append(layer_swap(across_two[2], 1))
        if layered and (which, step) == (1, 0):
            far_grads = [thirds(pair) for pair in expert_grads(kept[1])]
            last, far_grads = barrier((last, far_grads))
            three_sum.append(layer_swap(far_grads[1][0], 1))
        elif layered and turn == len(order) - 1:
            last, kept[0], three_sum[0] = barrier((last, kept[0], three_sum[0]))
            two_sum.append(to_owner(0))
            three_sum += [layer_swap(far_grads[1][at], 1) for at in (1, 2)]
        if layered and 0 <= turn - ring.steps - 1 < len(totals):
            at = turn - ring.steps - 1
            last, totals[at] = barrier((last, totals[at]))
            if at == len(totals) - 1:
                total = totals[at]
        mix_parts[step][0][-1] = last
        while next_step < ring.steps and len(back_parts[next_step][0]) == len(half_ids):
            more = () if total is None else (total,)
            total = ring.hop(ring.part_sum(*back_parts[next_step], *more).astype(bf16))
            totals.append(total)
            next_step += 1

    if layered:
        near_grads = [thirds(pair) for pair in expert_grads(kept[0])]
        total, near_grads, three_sum[1], three_sum[2] = barrier(
            (total, near_grads, three_sum[1], three_sum[2])
        )
        two_sum += [to_owner(1), to_owner(2)]
        next_sum += [layer_swap(near_grads[1][which], 1) for which in range(3)]
        back = ring.part_sum(*back_parts[0], total)
    else:
        back = ring.part_sum(*back_parts[0], total)
        whole_grads = expert_grads(kept[0])
        back, whole_grads = barrier((back, whole_grads))
    normed_slope = back[:tokens]
    gate_slope = back[tokens : tokens + EXPERTS] + back[tokens + EXPERTS :]

    logits = lax.dot_general(
        router_weight, normed_two, (((0,), (1,)), ((), ())), preferred_element_type=f32
    )
    kept_logits = jnp.where(picks, logits, masked_score)
    powered = jnp.where(
        picks, jnp.exp(kept_logits - jnp.max(kept_logits, axis=0, keepdims=True)), 0.0
    )
    gates = powered / jnp.sum(powered, axis=0, keepdims=True)
    mean_slope = jnp.sum(gates * gate_slope, axis=0, keepdims=True)
    logit_slope = (gates * (gate_slope - mean_slope)).astype(bf16)
    router_grad = dot(logit_slope, normed_two)
    normed_slope = normed_slope + lax.dot_general(
        logit_slope, router_weight, (((0,), (1,)), ((), ())), preferred_element_type=f32
    )

    def mix_hop(step, total):
        more = () if total is None else (total,)
        return ring.hop(ring.part_sum(*mix_parts[step], *more).astype(bf16))

    expert_gain_grad = jnp.sum(normed_slope * base_two, axis=0)
    scaled_two = normed_slope * expert_gain
    residual_slope = (
        slope
        + second_scale * scaled_two
        - base_two
        * second_scale
        * second_scale
        * jnp.mean(scaled_two * residual, axis=-1, keepdims=True)
    )
    branch_slope = residual_slope.astype(bf16)
    output_grad = lax.dot_general(
        attended, branch_slope, (((0,), (0,)), ((), ())), preferred_element_type=f32
    ).astype(bf16)
    attended_slope = jnp.einsum(
        "sd,cd->sc", branch_slope, output_full, preferred_element_type=f32
    ).astype(bf16)
    output_owned = lax.psum_scatter(output_grad, "shard", scatter_dimension=0, tiled=True)

    attended_slope, mix_parts = barrier((attended_slope, mix_parts))
    mix = mix_hop(1, None)
    slopes_out = []
    mix_step = 2
    for part in range(2):
        if part > 0:
            attended_slope, mix = barrier((attended_slope, mix))
            if mix_step < ring.steps:
                mix = mix_hop(mix_step, mix)
                mix_step += 1
        if layered:
            attended_slope, next_sum[part] = barrier((attended_slope, next_sum[part]))
            if part == 1:
                attended_slope, two_sum[0] = barrier((attended_slope, two_sum[0]))
                finish(0)
        queries, keys, values, _, log_totals = heads[part]
        slopes_out.append(
            attention_backward(
                lengths, queries, keys, values, attended_slope, log_totals, cosine, sine, part
            )
        )
        if part == 0:
            attended_slope, slopes_out[0] = barrier((attended_slope, slopes_out[0]))
    pre_slopes = jnp.concatenate(
        [slopes_out[part][which] for which in range(3) for part in range(2)], axis=1
    )
    pre_slopes, mix = barrier((pre_slopes, mix))
    if layered:
        pre_slopes, next_sum[2], two_sum[1] = barrier((pre_slopes, next_sum[2], two_sum[1]))
        finish(1)
    while mix_step < ring.steps:
        mix = mix_hop(mix_step, mix)
        mix_step += 1
    input_grad = lax.dot_general(
        normed_one, pre_slopes, (((0,), (0,)), ((), ())), preferred_element_type=f32
    ).astype(bf16)
    input_owned = lax.psum_scatter(input_grad, "shard", scatter_dimension=0, tiled=True)
    normed_one_slope = jnp.einsum(
        "sc,dc->sd", pre_slopes, packed_full, preferred_element_type=f32
    )
    attention_gain_grad = jnp.sum(normed_one_slope * base_one, axis=0)
    gain_sum = jnp.concatenate(
        [attention_gain_grad[None], expert_gain_grad[None], router_grad], axis=0
    )
    for axis, size in (("rep", reps), ("shard", shards)):
        far_bit = 1
        while far_bit < size:
            gain_sum = gain_sum + lax.ppermute(
                gain_sum, axis, [(place, place ^ far_bit) for place in range(size)]
            )
            far_bit *= 2
    scaled_one = normed_one_slope * attention_gain
    input_slope = (
        residual_slope
        + first_scale * scaled_one
        - base_one
        * first_scale
        * first_scale
        * jnp.mean(scaled_one * inputs_f, axis=-1, keepdims=True)
    )
    input_gradient = input_slope.astype(bf16)
    if layered:
        input_gradient, two_sum[2] = barrier((input_gradient, two_sum[2]))
        finish(2)
    layer_output = (residual + ring.part_sum(*mix_parts[0], mix)).astype(bf16)

    def rep_sum(*arrays):
        if reps != 2:
            return lax.psum(tuple(array.astype(f32) for array in arrays), "rep")
        low = [array.astype(bf16) for array in arrays]
        return tuple(a.astype(f32) + across(a).astype(f32) for a in low)

    if layered:
        whole = [
            jnp.stack([jnp.where(rep == 0, a, b), jnp.where(rep == 0, b, a)])
            for a, b in zip([x.astype(f32) for x in sums], [x.astype(f32) for x in others])
        ]
        in_sum, down_sum = jnp.concatenate(whole[:2], axis=1), whole[2]
    else:
        in_sum, down_sum = rep_sum(
            jnp.stack([g[0] for g in whole_grads]), jnp.stack([g[1] for g in whole_grads])
        )
    gain_sum, output_owned, input_owned = barrier((gain_sum, output_owned, input_owned))
    output_sum, input_sum = rep_sum(output_owned, input_owned)
    return (
        layer_output,
        input_gradient,
        gain_sum[0],
        input_sum[:, : HEADS * HD],
        input_sum[:, HEADS * HD : (HEADS + KV) * HD],
        input_sum[:, (HEADS + KV) * HD :],
        output_sum,
        gain_sum[1],
        gain_sum[2:].T,
        in_sum[..., :half],
        in_sum[..., half:],
        down_sum,
    )


def solution(mesh):
    return jax.shard_map(
        functools.partial(on_device, mesh.shape["shard"], mesh.shape["rep"]),
        mesh=mesh,
        in_specs=(
            P(("shard", "rep"), None),
            P(),
            P("shard", None),
            P("shard", None),
            P("shard", None),
            P("shard", None),
            P(),
            P(),
            P("shard", None, None),
            P("shard", None, None),
            P("shard", None, None),
            P(("shard", "rep")),
            P(("shard", "rep"), None),
            P(("shard", "rep"), None),
        ),
        out_specs=(
            P(("shard", "rep"), None),
            P(("shard", "rep"), None),
            P(),
            P("shard", None),
            P("shard", None),
            P("shard", None),
            P("shard", None),
            P(),
            P(),
            P("shard", None, None),
            P("shard", None, None),
            P("shard", None, None),
        ),
        check_vma=False,
    )
```

```python
import functools

import jax
import jax.numpy as jnp
import numpy as np
from jax import lax
from jax.experimental import pallas as pl
from jax.experimental.pallas import tpu as pltpu
from jax.sharding import PartitionSpec as P

D = 1024
HEADS = 16
KV = 8
HD = 64
EXPERTS = 32
TOP = 8
CAP = 288
ABSENT = -100000


epsilon = 1e-06
masked_score = -1e30
rotary_base = 10000.0


def chip_cycle(count):
    if count % 4 == 0 and count >= 8:
        wide = count // 4
        tall = 4
    else:
        return list(range(count))
    if wide == 1:
        return list(range(count))
    order = [row * wide for row in range(tall)]
    for step, row in enumerate(reversed(range(tall))):
        columns = range(1, wide) if step % 2 == 0 else reversed(range(1, wide))
        order += [row * wide + column for column in columns]
    return order


class Ring:
    def __init__(self, shards, reps, layers):
        if layers > 1:
            wide = shards // (2 * layers)
            cells = [
                [(layer * wide + x, y) for y in range(reps) for x in (range(wide) if y % 2 == 0 else reversed(range(wide)))]
                for layer in range(layers)
            ]
        else:
            cells = [[(chip, rep) for chip in chip_cycle(shards // 2)] for rep in range(reps)]
        self.steps = len(cells[0])
        self.forward, self.swap = [], []

        def device(chip, core):
            return (2 * chip[0] + core) * reps + chip[1]

        for cell in cells:
            for place, here in enumerate(cell):
                there = cell[(place + 1) % len(cell)]
                self.forward += [
                    (device(here, 0), device(there, 0)),
                    (device(there, 1), device(here, 1)),
                ]
                self.swap += [(device(here, 0), device(here, 1)), (device(here, 1), device(here, 0))]

    def hop(self, array):
        return lax.ppermute(array, ("shard", "rep"), self.forward)

    def cross(self, array):
        return lax.ppermute(array, ("shard", "rep"), self.swap)

    def part_sum(self, near, far, *more):
        far = far[0] if len(far) == 1 else sum(part.astype(jnp.float32) for part in far)
        parts = [*near, self.cross(far.astype(jnp.bfloat16)), *more]
        return sum(part.astype(jnp.float32) for part in parts)


def rope_tables(tokens):
    halfway = HD // 2
    index_float = jnp.arange(halfway, dtype=jnp.float32)
    frequency = jnp.exp(-jnp.log(rotary_base) * index_float * 2.0 / HD)
    angle = jnp.arange(tokens, dtype=jnp.float32)[:, None] * frequency[None, :]
    cosine, sine = jnp.cos(angle), jnp.sin(angle)
    return (
        jnp.concatenate([cosine] * 4, axis=1),
        jnp.concatenate([-sine, sine, -sine, sine], axis=1),
    )


def dot(l,r): return jnp.dot(l,r,preferred_element_type=jnp.float32)
def dot_nt(l,r): return lax.dot_general(l,r,(((1,),(1,)),((),())),preferred_element_type=jnp.float32)
def dot_tn(l,r): return lax.dot_general(l,r,(((0,),(0,)),((),())),preferred_element_type=jnp.float32)

def swap_halves(values):
    parts=[]
    for start in range(0, values.shape[1], 128):
        part=values[:,start:start+128]
        lane=lax.broadcasted_iota(jnp.int32,part.shape,1)
        parts.append(jnp.where(lane % HD < HD//2, pltpu.roll(part,128-HD//2,1), pltpu.roll(part,HD//2,1)))
    return parts[0] if len(parts)==1 else jnp.concatenate(parts,axis=1)

def tile(table,width):
    return table if width==128 else jnp.concatenate([table]*(width//128),axis=1)

def forward_kernel(block, length_ref, normed_ref, wq_ref, wk_ref, wv_ref, cos_ref, sin_ref,
                   q_ref,k_ref,v_ref,out_ref,total_ref):
    tokens=normed_ref.shape[0]
    length=length_ref[0]
    cos,sin=cos_ref[...],sin_ref[...]
    bf16=jnp.bfloat16
    x=normed_ref[...]
    q=dot(x,wq_ref[...])
    q=q*tile(cos,q.shape[1])+swap_halves(q)*tile(sin,q.shape[1])
    q_ref[...]=(q.astype(bf16).astype(jnp.float32)*(HD**-0.5)).astype(bf16)
    k=dot(x,wk_ref[...])
    k_ref[...]=(k*cos+swap_halves(k)*sin).astype(bf16)
    v_ref[...]=dot(x,wv_ref[...]).astype(bf16)
    groups=HEADS//KV
    for head in range(2):
        for i in range(tokens//block):
            rows=slice(i*block,(i+1)*block)
            span=(i+1)*block
            keys=k_ref[:span,head*HD:(head+1)*HD]
            vals=v_ref[:span,head*HD:(head+1)*HD]
            qs=jnp.concatenate([q_ref[rows,(head*groups+h)*HD:(head*groups+h+1)*HD] for h in range(groups)],axis=0)
            s=dot_nt(keys,qs)
            key_place=lax.broadcasted_iota(jnp.int32,s.shape,0)
            query_place=lax.broadcasted_iota(jnp.int32,s.shape,1) % block + i*block
            s=jnp.where(key_place<=jnp.minimum(query_place,length-1),s,masked_score)
            top=jnp.max(s,axis=0,keepdims=True)
            p=jnp.exp(s-top)
            total=jnp.sum(p,axis=0,keepdims=True)
            p=(p*(1.0/total)).astype(bf16)
            o=dot_tn(p,vals)
            log_total=top+jnp.log(total)
            for h in range(groups):
                at=head*groups+h
                out_ref[rows,at*HD:(at+1)*HD]=o[h*block:(h+1)*block].astype(bf16)
                total_ref[0,at:at+1,rows]=log_total[:,h*block:(h+1)*block]

def attention_forward(length, normed, packed, cos, sin, part, block=256):
    tokens,width=normed.shape
    qw=HEADS*HD//4; kw=KV*HD//4
    bf16=jnp.bfloat16
    qb=HEADS*HD//kw; vb=(HEADS+KV)*HD//kw
    return pl.pallas_call(
        functools.partial(forward_kernel,block),
        out_shape=[jax.ShapeDtypeStruct((tokens,2*qw),bf16),jax.ShapeDtypeStruct((tokens,2*kw),bf16),jax.ShapeDtypeStruct((tokens,2*kw),bf16),
                   jax.ShapeDtypeStruct((tokens,2*qw),bf16),jax.ShapeDtypeStruct((2,HEADS//4,tokens),jnp.float32)],
        grid_spec=pltpu.PrefetchScalarGridSpec(num_scalar_prefetch=1,grid=(2,),
            in_specs=[pl.BlockSpec((tokens,width),lambda g,l:(0,0)),
                      pl.BlockSpec((width,qw),lambda g,l:(0,g+2*part)),
                      pl.BlockSpec((width,kw),lambda g,l:(0,qb+g+2*part)),
                      pl.BlockSpec((width,kw),lambda g,l:(0,vb+g+2*part)),
                      pl.BlockSpec((tokens,128),lambda g,l:(0,0)),pl.BlockSpec((tokens,128),lambda g,l:(0,0))],
            out_specs=[pl.BlockSpec((tokens,qw),lambda g,l:(0,g)),pl.BlockSpec((tokens,kw),lambda g,l:(0,g)),pl.BlockSpec((tokens,kw),lambda g,l:(0,g)),
                       pl.BlockSpec((tokens,qw),lambda g,l:(0,g)),pl.BlockSpec((1,HEADS//4,tokens),lambda g,l:(g,0,0))]),
        compiler_params=pltpu.CompilerParams(vmem_limit_bytes=40*1024*1024),
        cost_estimate=pl.CostEstimate(flops=30*10**9,bytes_accessed=20*1024*1024,transcendentals=0),
    )(length,normed,packed,packed,packed,cos,sin)

def backward_kernel(block,length_ref,q_ref,k_ref,v_ref,slope_ref,total_ref,cos_ref,sin_ref,dq_ref,dk_ref,dv_ref,dq_s,dk_s,dv_s):
    tokens=q_ref.shape[0]
    length=length_ref[0]
    bf16=jnp.bfloat16
    groups=HEADS//KV
    for head in range(2):
        lanes=slice(head*HD,(head+1)*HD)
        for i in reversed(range(tokens//block)):
            rows=slice(i*block,(i+1)*block)
            span=(i+1)*block
            keys=k_ref[:span,lanes]; vals=v_ref[:span,lanes]
            heads=[slice((head*groups+h)*HD,(head*groups+h+1)*HD) for h in range(groups)]
            qs=jnp.concatenate([q_ref[rows,at] for at in heads],axis=0)
            slopes=jnp.concatenate([slope_ref[rows,at] for at in heads],axis=0)
            log_total=jnp.concatenate([total_ref[0,head*groups+h:head*groups+h+1,rows] for h in range(groups)],axis=1)
            s=dot_nt(keys,qs)
            key_place=lax.broadcasted_iota(jnp.int32,s.shape,0)
            query_place=lax.broadcasted_iota(jnp.int32,s.shape,1) % block + i*block
            s=jnp.where(key_place<=jnp.minimum(query_place,length-1),s,masked_score)
            w=jnp.exp(s-log_total)
            ps=dot_nt(vals,slopes)
            centre=jnp.sum(w*ps,axis=0,keepdims=True)
            ds=(w*(ps-centre)).astype(bf16)
            dq=dot_tn(ds,keys)
            dk=dot(ds,qs)
            dv=dot(w.astype(bf16),slopes)
            for h in range(groups):
                dq_s[rows,heads[h]]=dq[h*block:(h+1)*block]*(HD**-0.5)
            if i==tokens//block-1:
                dk_s[:,lanes]=dk; dv_s[:,lanes]=dv
            else:
                dk_s[:span,lanes]+=dk; dv_s[:span,lanes]+=dv
    cos,sin=cos_ref[...],sin_ref[...]
    dq=dq_s[...]
    dq_ref[...]=(dq*tile(cos,dq.shape[1])-swap_halves(dq)*tile(sin,dq.shape[1])).astype(bf16)
    dk=dk_s[...]
    dk_ref[...]=(dk*cos-swap_halves(dk)*sin).astype(bf16)
    dv_ref[...]=dv_s[...].astype(bf16)

def attention_backward(length,q,k,v,slope,total,cos,sin,part,block=256):
    tokens=q.shape[0]
    qw=HEADS*HD//4; kw=KV*HD//4
    bf16=jnp.bfloat16
    qs=pl.BlockSpec((tokens,qw),lambda g,l:(0,g)); ks=pl.BlockSpec((tokens,kw),lambda g,l:(0,g)); cs=pl.BlockSpec((tokens,128),lambda g,l:(0,0))
    return pl.pallas_call(
        functools.partial(backward_kernel,block),
        out_shape=[jax.ShapeDtypeStruct((tokens,2*qw),bf16),jax.ShapeDtypeStruct((tokens,2*kw),bf16),jax.ShapeDtypeStruct((tokens,2*kw),bf16)],
        grid_spec=pltpu.PrefetchScalarGridSpec(num_scalar_prefetch=1,grid=(2,),
            in_specs=[qs,ks,ks,pl.BlockSpec((tokens,qw),lambda g,l:(0,g+2*part)),pl.BlockSpec((1,HEADS//4,tokens),lambda g,l:(g,0,0)),cs,cs],
            out_specs=[qs,ks,ks],
            scratch_shapes=[pltpu.VMEM((tokens,qw),jnp.float32),pltpu.VMEM((tokens,kw),jnp.float32),pltpu.VMEM((tokens,kw),jnp.float32)]),
        compiler_params=pltpu.CompilerParams(vmem_limit_bytes=40*1024*1024),
        cost_estimate=pl.CostEstimate(flops=20*10**9,bytes_accessed=10*1024*1024,transcendentals=0),
    )(length,q,k,v,slope,total,cos,sin)

def pair_kernel(
    count,
    step,
    chained,
    ids_ref,
    tokens_a,
    tokens_b,
    slope_a,
    slope_b,
    row_a,
    row_b,
    mask_a,
    mask_b,
    router_ref,
    *rest,
):
    weights, rest = rest[: 3 * count], rest[3 * count :]
    rest = rest[4:] if chained else rest
    back_out, mix_out, kept_out, rest = rest[0:2], rest[2:4], rest[4:8], rest[8:]
    blocks, backs, mixes, gates_in, ups_in, downs_in, rest = *rest[:6], rest[6:]
    rows_buf, routed_buf, hidden_buf, slopes_buf, raw_buf, mixed_rows, back_rows, rest = (
        *rest[:7],
        rest[7:],
    )
    load_sems, weight_sems, back_sems, mix_sems, kept_sems = rest
    tokens = blocks.shape[1]
    pair_rows = 2 * CAP
    bf16, f32 = jnp.bfloat16, jnp.float32
    sources = (tokens_a, slope_a, tokens_b, slope_b)

    def load(which):
        return pltpu.make_async_copy(
            sources[which].at[pl.ds(0, tokens)], blocks.at[which], load_sems.at[which]
        )

    def load_weight(e, which):
        target = (gates_in, ups_in, downs_in)[which].at[e]
        return pltpu.make_async_copy(weights[3 * e + which], target, weight_sems.at[e, which])

    stores = []

    def store(source, target, sem):
        stores.append(pltpu.make_async_copy(source, target, sem))
        stores[-1].start()

    def keep(e, which):
        source = (rows_buf, routed_buf, hidden_buf, slopes_buf)[which].at[e]
        target = kept_out[which].at[e, pl.ds(step * pair_rows, pair_rows)]
        store(source, target, kept_sems.at[e, which])

    for which in (0, 2, 1, 3):
        load(which).start()
    for e in range(count):
        for which in range(3):
            load_weight(e, which).start()

    taken, picks, chosen = [], [], []
    for side, (row_ref, mask_ref) in enumerate(((row_a, mask_a), (row_b, mask_b))):
        place = lax.broadcasted_iota(jnp.int32, (CAP, tokens), 0)
        taken.append([row_ref[0, e : e + 1] == place for e in range(count)])
        hits = [jnp.where(hit, 1.0, 0.0).astype(bf16) for hit in taken[side]]
        picks.append(hits[0] if count == 1 else jnp.concatenate(hits, axis=0))
        chosen.append(dot_nt(picks[side], mask_ref[...]))
        load(2 * side).wait()
        rows = dot(picks[side], blocks[2 * side]).astype(bf16)
        for e in range(count):
            rows_buf[e, side * CAP : (side + 1) * CAP] = rows[e * CAP : (e + 1) * CAP]
    for e in range(count):
        keep(e, 0)
    for side in range(2):
        load(2 * side + 1).wait()
        rows = dot(picks[side], blocks[2 * side + 1]).astype(bf16)
        for e in range(count):
            raw_buf[e, side * CAP : (side + 1) * CAP] = rows[e * CAP : (e + 1) * CAP]
    homeward = [[], []]
    for e in range(count):
        rows = rows_buf[e]
        marks = jnp.concatenate([chosen[side][e * CAP : (e + 1) * CAP] for side in range(2)], axis=0)
        logits = dot(rows, router_ref[...])
        kept = jnp.where(marks > 0.5, logits, masked_score)
        top = jnp.max(kept, axis=-1, keepdims=True)
        powered = jnp.exp(kept - top) * marks
        total = jnp.sum(powered, axis=-1, keepdims=True)
        lane = lax.broadcasted_iota(jnp.int32, powered.shape, 1)
        mine = lane == ids_ref[e]
        gate = jnp.sum(jnp.where(mine, powered, 0.0), axis=-1, keepdims=True) / jnp.where(
            total > 0.0, total, 1.0
        )
        slope_rows = raw_buf[e].astype(f32)
        routed = (gate * slope_rows).astype(bf16)
        routed_buf[e] = routed
        keep(e, 1)
        for which in range(3):
            load_weight(e, which).wait()
        gate_part = dot(rows, gates_in[e])
        up_part = dot(rows, ups_in[e])
        hidden_slope = dot_nt(routed, downs_in[e])
        sigma = 1.0 / (1.0 + jnp.exp(-gate_part))
        silu = gate_part * sigma
        hidden = (silu * up_part).astype(bf16)
        hidden_buf[e] = hidden
        keep(e, 2)
        gate_back = (hidden_slope * up_part * sigma * (1.0 + gate_part * (1.0 - sigma))).astype(bf16)
        up_back = (hidden_slope * silu).astype(bf16)
        half = gate_back.shape[1]
        slopes_buf[e, :, :half] = gate_back
        slopes_buf[e, :, half:] = up_back
        keep(e, 3)
        out = dot(hidden, downs_in[e]).astype(bf16).astype(f32)
        back = (dot_nt(gate_back, gates_in[e]) + dot_nt(up_back, ups_in[e])).astype(bf16)
        gate_slope = jnp.sum(out * slope_rows, axis=-1, keepdims=True)
        mixed = (gate * out).astype(bf16)
        for side in range(2):
            part = slice(side * CAP, (side + 1) * CAP)
            homeward[side].append(
                jnp.sum(jnp.where(taken[side][e], gate_slope[part], 0.0), axis=0, keepdims=True)
            )
            mixed_rows[side, e * CAP : (e + 1) * CAP] = mixed[part]
            back_rows[side, e * CAP : (e + 1) * CAP] = back[part]
    for side, row_ref in enumerate((row_a, row_b)):
        backs[side, :tokens] = dot_tn(picks[side], back_rows[side]).astype(bf16)
        row = lax.broadcasted_iota(jnp.int32, (EXPERTS, tokens), 0)
        whole = jnp.zeros(row.shape, f32)
        for e in range(count):
            whole = jnp.where(row == ids_ref[e], homeward[side][e], whole)
        high = whole.astype(bf16)
        backs[side, tokens : tokens + EXPERTS] = high
        backs[side, tokens + EXPERTS :] = (whole - high.astype(f32)).astype(bf16)
        store(backs.at[side], back_out[side], back_sems.at[side])
        mixes[side] = dot_tn(picks[side], mixed_rows[side]).astype(bf16)
        store(mixes.at[side], mix_out[side], mix_sems.at[side])
    for copy in stores:
        copy.wait()


def experts_pair(step, steps, expert_ids, ta, tb, sa, sb, slots, weights, kept):
    router, *weights = weights
    tokens, width = ta.shape
    count, half = len(weights) // 3, weights[2].shape[0]
    bf16 = jnp.bfloat16
    chained = kept is not None
    once = pl.Buffered(1)
    back_rows = tokens + 2 * EXPERTS

    def block(rows, at=0):
        return pl.BlockSpec((rows, width), lambda e, w: (at, 0), pipeline_mode=once)

    anywhere = pl.BlockSpec(memory_space=pl.ANY)
    in_specs = [anywhere] * 4
    in_specs += [
        pl.BlockSpec((1, count, tokens), lambda e, w, i=i: (2 * step + i, 0, 0), pipeline_mode=once)
        for i in range(2)
    ]
    in_specs += [block(EXPERTS, tokens // EXPERTS)] * 2
    in_specs += [pl.BlockSpec((width, EXPERTS), lambda e, w: (0, 0), pipeline_mode=once)]
    in_specs += [anywhere] * len(weights)
    rows = 2 * CAP
    columns = (width, width, half, 2 * half)
    shapes = [jax.ShapeDtypeStruct((back_rows, width), bf16)] * 2
    shapes += [jax.ShapeDtypeStruct((tokens, width), bf16)] * 2
    shapes += [jax.ShapeDtypeStruct((count, steps * rows, column), bf16) for column in columns]
    out_specs = [anywhere] * 8
    operands = [ta, tb, sa, sb, slots, slots, sa, sb, router, *weights]
    aliases = {}
    if chained:
        first = 1 + len(operands)
        operands += list(kept)
        in_specs += [anywhere] * 4
        aliases = {first + p: 4 + p for p in range(4)}
    flops = count * 2 * rows * (4 * tokens * width + 6 * width * half)
    return pl.pallas_call(
        functools.partial(pair_kernel, count, step, chained),
        out_shape=shapes,
        grid_spec=pltpu.PrefetchScalarGridSpec(
            num_scalar_prefetch=1,
            grid=(1,),
            in_specs=in_specs,
            out_specs=out_specs,
            scratch_shapes=[
                pltpu.VMEM((4, tokens, width), bf16),
                pltpu.VMEM((2, back_rows, width), bf16),
                pltpu.VMEM((2, tokens, width), bf16),
                pltpu.VMEM((count, width, half), bf16),
                pltpu.VMEM((count, width, half), bf16),
                pltpu.VMEM((count, half, width), bf16),
                *[pltpu.VMEM((count, rows, column), bf16) for column in columns],
                pltpu.VMEM((count, rows, width), bf16),
                pltpu.VMEM((2, count * CAP, width), bf16),
                pltpu.VMEM((2, count * CAP, width), bf16),
                pltpu.SemaphoreType.DMA((4,)),
                pltpu.SemaphoreType.DMA((count, 3)),
                pltpu.SemaphoreType.DMA((2,)),
                pltpu.SemaphoreType.DMA((2,)),
                pltpu.SemaphoreType.DMA((count, 4)),
            ],
        ),
        input_output_aliases=aliases,
        compiler_params=pltpu.CompilerParams(vmem_limit_bytes=60 * 1024 * 1024),
        cost_estimate=pl.CostEstimate(
            flops=2 * flops, bytes_accessed=40 * 1024 * 1024, transcendentals=0
        ),
    )(expert_ids, *operands)


def on_device(
    shards,
    reps,
    layer_input,
    attention_gain,
    query_weight,
    key_weight,
    value_weight,
    output_weight,
    expert_gain,
    router_weight,
    gate_weight,
    up_weight,
    down_weight,
    lengths,
    routes,
    cotangent,
):
    me, rep = lax.axis_index("shard"), lax.axis_index("rep")
    tokens = layer_input.shape[0]
    local_experts, half = down_weight.shape[0], down_weight.shape[1]
    length = lengths[0]
    bf16, f32 = jnp.bfloat16, jnp.float32
    heads_width = (HEADS + 2 * KV) * HD
    layers = 4 if (shards == 16 and reps == 2 and local_experts == 2) else 1
    layered = layers > 1
    ring = Ring(shards, reps, layers)
    barrier = lax.optimization_barrier

    packed = jnp.concatenate([query_weight, key_weight, value_weight], axis=1)
    packed_full = lax.all_gather(packed, "shard", axis=0, tiled=True)
    packed_full, output_weight = barrier((packed_full, output_weight))
    output_full = lax.all_gather(output_weight, "shard", axis=0, tiled=True)

    def layer_swap(array, bit):
        stride = bit * (shards // layers)
        return lax.ppermute(array, "shard", [(s, s ^ stride) for s in range(shards)])

    if layered:
        own = [
            lax.dynamic_index_in_dim(weight, rep, axis=0, keepdims=False)
            for weight in (gate_weight, up_weight, down_weight)
        ]

        def owned(bits):
            return 2 * (me ^ (bits * (shards // layers))) + rep

        half_ids = [
            jnp.stack([owned(0), owned(1)]).astype(jnp.int32),
            jnp.stack([owned(2), owned(3)]).astype(jnp.int32),
        ]
    else:
        half_ids = [(me * local_experts + jnp.arange(local_experts)).astype(jnp.int32)]

    expert_ids = jnp.arange(EXPERTS, dtype=jnp.int32)
    routes_turned = routes.T
    picks = functools.reduce(
        jnp.logical_or, [routes_turned[k][None, :] == expert_ids[:, None] for k in range(TOP)]
    )
    valid = (jnp.arange(tokens, dtype=jnp.int32) < length)[:, None]
    slope_low = jnp.where(valid, cotangent, jnp.zeros_like(cotangent))
    slope = slope_low.astype(f32)
    slope_near = [jnp.concatenate([slope_low, picks.astype(bf16)], axis=0)]

    def slope_hop(*tie):
        if len(slope_near) == ring.steps:
            return tie
        arrived = ring.hop(slope_near[-1])
        arrived, *tie = barrier((arrived, *tie))
        slope_near.append(arrived)
        return tie

    inputs_f = layer_input.astype(f32)
    first_scale = lax.rsqrt(jnp.mean(inputs_f * inputs_f, axis=-1, keepdims=True) + epsilon)
    base_one = inputs_f * first_scale
    normed_one = (base_one * attention_gain).astype(bf16)
    cosine, sine = rope_tables(tokens)
    (normed_one,) = slope_hop(normed_one)
    normed_one, packed_full = slope_hop(normed_one, packed_full)
    if layered:
        packed_full, own = barrier((packed_full, own))
        next_one = [layer_swap(own[0], 1)]
        across_two = [layer_swap(own[0], 2)]
    heads = []
    for part in range(2):
        result = attention_forward(lengths, normed_one, packed_full, cosine, sine, part)
        if part == 0:
            result, packed_full = slope_hop(result, packed_full)
            if layered:
                result, packed_full, own, next_one[0] = barrier(
                    (result, packed_full, own, next_one[0])
                )
                next_one.append(layer_swap(own[1], 1))
        elif layered:
            result, own, next_one[1], across_two[0] = barrier(
                (result, own, next_one[1], across_two[0])
            )
            next_one.append(layer_swap(own[2], 1))
            across_two.append(layer_swap(own[1], 2))
        heads.append(result)
    attended = jnp.concatenate([heads[part][3] for part in range(2)], axis=1)
    residual = inputs_f + dot(attended, output_full)
    second_scale = lax.rsqrt(jnp.mean(residual * residual, axis=-1, keepdims=True) + epsilon)
    base_two = residual * second_scale
    normed_two = (base_two * expert_gain).astype(bf16)

    across_three = []
    if layered:
        normed_two, across_two[0], own = barrier((normed_two, across_two[0], own))
        across_two.append(layer_swap(own[2], 2))
        across_three.append(layer_swap(across_two[0], 1))

    near = [normed_two]
    while len(near) < ring.steps:
        near.append(ring.hop(near[-1]))
        if len(slope_near) < ring.steps:
            near[-1], *_ = slope_hop(near[-1])
    far = [ring.cross(block) for block in near]
    slope_far = [ring.cross(block) for block in slope_near]

    masks = jnp.stack(
        [block[tokens:] for step in range(ring.steps) for block in (slope_near[step], slope_far[step])]
    )
    earlier = jnp.triu(jnp.ones((tokens, tokens), bf16), k=1)
    all_ids = jnp.concatenate(half_ids)
    mine = jnp.take(masks.astype(f32), all_ids, axis=1, mode="clip")
    ranks = dot(mine.reshape(-1, tokens).astype(bf16), earlier).astype(jnp.int32).reshape(mine.shape)
    slots = jnp.where(mine > 0.5, ranks, ABSENT)
    count = half_ids[0].shape[0]
    half_slots = [slots[:, h * count : (h + 1) * count] for h in range(len(half_ids))]

    if layered:
        order = [(0, step) for step in range(ring.steps - 1)]
        order += [(1, step % ring.steps) for step in range(1, ring.steps + 1)]
        order += [(0, ring.steps - 1)]
    else:
        half_weights = [
            [w[e] for e in range(local_experts) for w in (gate_weight, up_weight, down_weight)]
        ]
        order = [(0, step) for step in range(ring.steps)]

    def expert_grads(kept):
        rows, routed, hidden, slopes = kept
        turned = (((0,), (0,)), ((), ()))
        return [
            (
                lax.dot_general(rows[e], slopes[e], turned, preferred_element_type=f32).astype(bf16),
                lax.dot_general(hidden[e], routed[e], turned, preferred_element_type=f32).astype(bf16),
            )
            for e in range(count)
        ]

    def thirds(pair):
        middle = pair[0].shape[0] // 2
        return [pair[0][:middle], pair[0][middle:], pair[1]]

    def to_owner(which):
        both = far_grads[0][which].astype(f32) + three_sum[which].astype(f32)
        return layer_swap(both.astype(bf16), 2)

    def across(array):
        return lax.ppermute(array, "rep", [(0, 1), (1, 0)])

    def finish(which):
        parts = (near_grads[0][which], two_sum[which], next_sum[which])
        sums.append(sum(g.astype(f32) for g in parts).astype(bf16))
        others.append(across(sums[-1]))

    three_sum, next_sum, two_sum, sums, others = [], [], [], [], []
    kept = [None] * len(half_ids)
    back_parts = [([], []) for _ in range(ring.steps)]
    mix_parts = [([], []) for _ in range(ring.steps)]
    total, totals, next_step, last = None, [], 1, None
    for turn, (which, step) in enumerate(order):
        tokens_now = near[step]
        if last is not None:
            tokens_now, last = barrier((tokens_now, last))
        if layered:
            now = [*own, *next_one] if which == 0 else [*across_two, *across_three]
        else:
            now = half_weights[0]
        results = experts_pair(
            step,
            ring.steps,
            half_ids[which],
            tokens_now,
            far[step],
            slope_near[step],
            slope_far[step],
            half_slots[which],
            (router_weight, *now),
            kept[which],
        )
        kept[which] = results[4:8]
        for side in range(2):
            back_parts[step][side].append(results[side])
            mix_parts[step][side].append(results[2 + side])
        last = results[2]
        if layered and turn == 0:
            last, across_two[1], across_three[0] = barrier((last, across_two[1], across_three[0]))
            across_three.append(layer_swap(across_two[1], 1))
        elif layered and turn == 1:
            last, across_two[2], across_three[1] = barrier((last, across_two[2], across_three[1]))
            across_three.append(layer_swap(across_two[2], 1))
        if layered and (which, step) == (1, 0):
            far_grads = [thirds(pair) for pair in expert_grads(kept[1])]
            last, far_grads = barrier((last, far_grads))
            three_sum.append(layer_swap(far_grads[1][0], 1))
        elif layered and turn == len(order) - 1:
            last, kept[0], three_sum[0] = barrier((last, kept[0], three_sum[0]))
            two_sum.append(to_owner(0))
            three_sum += [layer_swap(far_grads[1][at], 1) for at in (1, 2)]
        if layered and 0 <= turn - ring.steps - 1 < len(totals):
            at = turn - ring.steps - 1
            last, totals[at] = barrier((last, totals[at]))
            if at == len(totals) - 1:
                total = totals[at]
        mix_parts[step][0][-1] = last
        while next_step < ring.steps and len(back_parts[next_step][0]) == len(half_ids):
            more = () if total is None else (total,)
            total = ring.hop(ring.part_sum(*back_parts[next_step], *more).astype(bf16))
            totals.append(total)
            next_step += 1

    if layered:
        near_grads = [thirds(pair) for pair in expert_grads(kept[0])]
        total, near_grads, three_sum[1], three_sum[2] = barrier(
            (total, near_grads, three_sum[1], three_sum[2])
        )
        two_sum += [to_owner(1), to_owner(2)]
        next_sum += [layer_swap(near_grads[1][which], 1) for which in range(3)]
        back = ring.part_sum(*back_parts[0], total)
    else:
        back = ring.part_sum(*back_parts[0], total)
        whole_grads = expert_grads(kept[0])
        back, whole_grads = barrier((back, whole_grads))
    normed_slope = back[:tokens]
    gate_slope = back[tokens : tokens + EXPERTS] + back[tokens + EXPERTS :]

    logits = lax.dot_general(
        router_weight, normed_two, (((0,), (1,)), ((), ())), preferred_element_type=f32
    )
    kept_logits = jnp.where(picks, logits, masked_score)
    powered = jnp.where(
        picks, jnp.exp(kept_logits - jnp.max(kept_logits, axis=0, keepdims=True)), 0.0
    )
    gates = powered / jnp.sum(powered, axis=0, keepdims=True)
    mean_slope = jnp.sum(gates * gate_slope, axis=0, keepdims=True)
    logit_slope = (gates * (gate_slope - mean_slope)).astype(bf16)
    router_grad = dot(logit_slope, normed_two)
    normed_slope = normed_slope + lax.dot_general(
        logit_slope, router_weight, (((0,), (1,)), ((), ())), preferred_element_type=f32
    )

    def mix_hop(step, total):
        more = () if total is None else (total,)
        return ring.hop(ring.part_sum(*mix_parts[step], *more).astype(bf16))

    expert_gain_grad = jnp.sum(normed_slope * base_two, axis=0)
    scaled_two = normed_slope * expert_gain
    residual_slope = (
        slope
        + second_scale * scaled_two
        - base_two
        * second_scale
        * second_scale
        * jnp.mean(scaled_two * residual, axis=-1, keepdims=True)
    )
    branch_slope = residual_slope.astype(bf16)
    output_grad = lax.dot_general(
        attended, branch_slope, (((0,), (0,)), ((), ())), preferred_element_type=f32
    ).astype(bf16)
    attended_slope = jnp.einsum(
        "sd,cd->sc", branch_slope, output_full, preferred_element_type=f32
    ).astype(bf16)
    output_owned = lax.psum_scatter(output_grad, "shard", scatter_dimension=0, tiled=True)

    attended_slope, mix_parts = barrier((attended_slope, mix_parts))
    mix = mix_hop(1, None)
    slopes_out = []
    mix_step = 2
    for part in range(2):
        if part > 0:
            attended_slope, mix = barrier((attended_slope, mix))
            if mix_step < ring.steps:
                mix = mix_hop(mix_step, mix)
                mix_step += 1
        if layered:
            if part == 1:
                attended_slope, two_sum[0], next_sum[0] = barrier(
                    (attended_slope, two_sum[0], next_sum[0])
                )
                finish(0)
        queries, keys, values, _, log_totals = heads[part]
        slopes_out.append(
            attention_backward(
                lengths, queries, keys, values, attended_slope, log_totals, cosine, sine, part
            )
        )
        if part == 0:
            attended_slope, slopes_out[0] = barrier((attended_slope, slopes_out[0]))
    pre_slopes = jnp.concatenate(
        [slopes_out[part][which] for which in range(3) for part in range(2)], axis=1
    )
    pre_slopes, mix = barrier((pre_slopes, mix))
    if layered:
        pre_slopes, next_sum[1], two_sum[1] = barrier((pre_slopes, next_sum[1], two_sum[1]))
        finish(1)
    while mix_step < ring.steps:
        mix = mix_hop(mix_step, mix)
        mix_step += 1
    input_grad = lax.dot_general(
        normed_one, pre_slopes, (((0,), (0,)), ((), ())), preferred_element_type=f32
    ).astype(bf16)
    input_owned = lax.psum_scatter(input_grad, "shard", scatter_dimension=0, tiled=True)
    normed_one_slope = jnp.einsum(
        "sc,dc->sd", pre_slopes, packed_full, preferred_element_type=f32
    )
    attention_gain_grad = jnp.sum(normed_one_slope * base_one, axis=0)
    gain_sum = jnp.concatenate(
        [attention_gain_grad[None], expert_gain_grad[None], router_grad], axis=0
    )
    for axis, size in (("rep", reps), ("shard", shards)):
        far_bit = 1
        while far_bit < size:
            gain_sum = gain_sum + lax.ppermute(
                gain_sum, axis, [(place, place ^ far_bit) for place in range(size)]
            )
            far_bit *= 2
    scaled_one = normed_one_slope * attention_gain
    input_slope = (
        residual_slope
        + first_scale * scaled_one
        - base_one
        * first_scale
        * first_scale
        * jnp.mean(scaled_one * inputs_f, axis=-1, keepdims=True)
    )
    input_gradient = input_slope.astype(bf16)
    if layered:
        input_gradient, two_sum[2], next_sum[2], mix = barrier(
            (input_gradient, two_sum[2], next_sum[2], mix)
        )
        finish(2)
    layer_output = (residual + ring.part_sum(*mix_parts[0], mix)).astype(bf16)

    def rep_sum(*arrays):
        if reps != 2:
            return lax.psum(tuple(array.astype(f32) for array in arrays), "rep")
        low = [array.astype(bf16) for array in arrays]
        return tuple(a.astype(f32) + across(a).astype(f32) for a in low)

    if layered:
        whole = [
            jnp.stack([jnp.where(rep == 0, a, b), jnp.where(rep == 0, b, a)])
            for a, b in zip([x.astype(f32) for x in sums], [x.astype(f32) for x in others])
        ]
        in_sum, down_sum = jnp.concatenate(whole[:2], axis=1), whole[2]
    else:
        in_sum, down_sum = rep_sum(
            jnp.stack([g[0] for g in whole_grads]), jnp.stack([g[1] for g in whole_grads])
        )
    gain_sum, output_owned, input_owned = barrier((gain_sum, output_owned, input_owned))
    output_sum, input_sum = rep_sum(output_owned, input_owned)
    return (
        layer_output,
        input_gradient,
        gain_sum[0],
        input_sum[:, : HEADS * HD],
        input_sum[:, HEADS * HD : (HEADS + KV) * HD],
        input_sum[:, (HEADS + KV) * HD :],
        output_sum,
        gain_sum[1],
        gain_sum[2:].T,
        in_sum[..., :half],
        in_sum[..., half:],
        down_sum,
    )


def solution(mesh):
    return jax.shard_map(
        functools.partial(on_device, mesh.shape["shard"], mesh.shape["rep"]),
        mesh=mesh,
        in_specs=(
            P(("shard", "rep"), None),
            P(),
            P("shard", None),
            P("shard", None),
            P("shard", None),
            P("shard", None),
            P(),
            P(),
            P("shard", None, None),
            P("shard", None, None),
            P("shard", None, None),
            P(("shard", "rep")),
            P(("shard", "rep"), None),
            P(("shard", "rep"), None),
        ),
        out_specs=(
            P(("shard", "rep"), None),
            P(("shard", "rep"), None),
            P(),
            P("shard", None),
            P("shard", None),
            P("shard", None),
            P("shard", None),
            P(),
            P(),
            P("shard", None, None),
            P("shard", None, None),
            P("shard", None, None),
        ),
        check_vma=False,
    )
```
